32 devices in a mesh: grp: 4 (over y, x), tm: 8 (over z, core).
Axes of the slice: x: 2, y: 2, z: 4, core: 2. Of those that a mesh axis runs over, the one named last changes fastest.
Arguments:
- signal: bfloat16 [4, 1024, 512], P('grp', 'tm'), may hold values from -6 to 6
- damping: float32 [4, 1024], P('grp', 'tm'), may hold values from 0.25 to 1, as said below
- nu_log: float32 [1024], replicated, as said below
- theta: float32 [1024], replicated, may hold values from 0 to 0.63
- in_weight: bfloat16 [512, 2048], replicated, may hold values from -0.25 to 0.25
- out_weight: bfloat16 [512, 2048], replicated, may hold values from -0.125 to 0.125
- skip_gain: float32 [512], replicated, may hold values from 0.1 to 1.9
- cotangent: bfloat16 [4, 1024, 512], P('grp', 'tm'), may hold values from -6 to 6
Outputs:
- mixed: bfloat16 [4, 1024, 512], P('grp', 'tm')
- grad_signal: bfloat16 [4, 1024, 512], P('grp', 'tm')
- grad_in: float32 [512, 2048], P(('grp', 'tm'))
- grad_out: float32 [512, 2048], P(('grp', 'tm'))
The draws below stay inside these ranges and needn't reach their ends.
Inputs may be any that keep to these rules, and one draw needn't show every extreme that they name: damping is 1 except at a few time steps of each record. exp(nu_log) lies between 0.01 / 1024 and 1/30.
All inputs are finite; a program needn't handle non-finite values.
Results may differ from the reference program's by a relative error of at most 0.0034.
Values sent between devices are 32-bit elements; how exact they have to be, the bound alone decides.
A program may use at most 128 MiB of HBM per device.

```python
import math
import jax
import jax.numpy as jnp
from jax import lax

D = 512
N = 1024
TOK_DEV = 128
RECORD_COUNT = 4
TOKEN_STEPS = 1024


def draw_nu_log(key, part):
    leading_operand, trailing_operand, third = jax.random.split(key, 3)
    share = 0.5
    quick_pick = jax.random.uniform(leading_operand, (N,), jnp.float32) < share
    quick = jax.random.uniform(trailing_operand, (N,), jnp.float32, minval=1.0 / 50.0, maxval=1.0 / 30.0)
    slow_log = jax.random.uniform(third, (N,), jnp.float32, minval=math.log(0.01 / TOKEN_STEPS), maxval=math.log(1.0 / TOKEN_STEPS))
    return jnp.where(quick_pick, jnp.log(quick), slow_log).astype(jnp.float32)


def draw_damping(key, part):
    leading_operand, trailing_operand = jax.random.split(key, 2)
    pulse_count = 8
    position_list = jax.random.randint(leading_operand, (RECORD_COUNT, pulse_count), 0, TOKEN_STEPS)
    intensity_factor = jax.random.uniform(trailing_operand, (RECORD_COUNT, pulse_count), jnp.float32, minval=0.6, maxval=0.8)
    marks = position_list[:, :, None] == jnp.arange(TOKEN_STEPS, dtype=jnp.int32)[None, None, :]
    factors = jnp.where(marks, intensity_factor[:, :, None], 1.0)
    return jnp.prod(factors, axis=1).astype(jnp.float32)


def strengthened(drawn, rng, source, target, blocks, factor):
    def block_of(dim):
        return (jnp.arange(drawn.shape[dim]) // (drawn.shape[dim] // blocks)).reshape((-1,) + (1,) * (drawn.ndim - 1 - dim))

    one_side = jax.random.permutation(rng, blocks)[block_of(target)]
    far = (block_of(target) + blocks // 2) % blocks
    return jnp.where((block_of(source) == one_side) | (block_of(source) == far), factor * drawn, drawn)


def levels(stream_key, shape, cuts, low, top_value):
    level = 1.0
    for axis_at, parts in cuts:
        heights = jax.random.uniform(jax.random.fold_in(jax.random.fold_in(stream_key, 6), axis_at), (parts,), jnp.float32, low / len(cuts), top_value / len(cuts))
        level = level * jnp.repeat(jnp.exp(heights), shape[axis_at] // parts).reshape((-1,) + (1,) * (len(shape) - 1 - axis_at))
    return level


def normal_values(rng, extent, spread, most, pieces=(), held_as=jnp.bfloat16):
    values = spread * jax.random.normal(rng, extent, jnp.float32)
    if pieces:
        values = values * levels(rng, extent, pieces, -0.22, 0.18)
    return jnp.clip(values, -most, most).astype(held_as)


def bell_draw_with(key, dims, spread, limit, pieces, heavy, kind=jnp.bfloat16):
    drawn = spread * jax.random.normal(key, dims, jnp.float32)
    if pieces:
        drawn = drawn * levels(key, dims, pieces, -0.22, 0.18)
    return jnp.clip(strengthened(drawn, jax.random.fold_in(key, 3), *heavy), -limit, limit).astype(kind)


def setup_inputs(seed: int = 0) -> dict:
    key_of = jax.random.split(jax.random.key(seed), 9)
    signal = bell_draw_with(key_of[0], (RECORD_COUNT, TOKEN_STEPS, D), 1.0, 6.0, ((0, 4), (1, 8)), (1, 2, 8, 2.0))
    damping = draw_damping(jax.random.fold_in(key_of[8], 71), 0)
    nu_log = draw_nu_log(jax.random.fold_in(key_of[8], 71), 0)
    theta = jnp.clip(jax.random.uniform(key_of[3], (N,), jnp.float32, 0.0, 0.63), 0.0, 0.63)
    in_weight = normal_values(key_of[4], (D, 2 * N), D ** -0.5, 0.25)
    out_weight = normal_values(key_of[5], (D, 2 * N), (2 * N) ** -0.5, 0.125)
    skip_gain = jnp.clip(1.0 + 0.18 * jax.random.normal(key_of[6], (D,), jnp.float32), 0.1, 1.9)
    cotangent = bell_draw_with(key_of[7], (RECORD_COUNT, TOKEN_STEPS, D), 1.0, 6.0, ((0, 4), (1, 8)), (1, 2, 8, 2.0))
    return {"signal": signal, "damping": damping, "nu_log": nu_log, "theta": theta, "in_weight": in_weight, "out_weight": out_weight, "skip_gain": skip_gain, "cotangent": cotangent}


def combine(earlier, later):
    first_re, first_im, carry_re, carry_im = earlier
    second_re, second_im, next_re, next_im = later
    prod_re = second_re * first_re - second_im * first_im
    prod_im = second_re * first_im + second_im * first_re
    moved_re = second_re * carry_re - second_im * carry_im
    moved_im = second_re * carry_im + second_im * carry_re
    return (prod_re, prod_im, moved_re + next_re, moved_im + next_im)

def reference(signal, damping, nu_log, theta, in_weight, out_weight, skip_gain, cotangent):
    width = nu_log.shape[0]
    rate = jnp.exp(nu_log)
    magnitude = jnp.exp(-rate)
    lam_re = magnitude * jnp.cos(theta)
    lam_im = magnitude * jnp.sin(theta)
    scaling = jnp.sqrt(-jnp.expm1(-2.0 * rate))
    blocks = TOKEN_STEPS // TOK_DEV

    def record_pass(totals, record):
        sig_all, damp_all, up_all = record
        sig_blocks = sig_all.reshape(blocks, TOK_DEV, D)
        damp_blocks = damp_all.reshape(blocks, TOK_DEV)
        up_blocks = up_all.reshape(blocks, TOK_DEV, D)

        def forward(carry, block):
            sig, damp, upstream = block
            decay_re = damp[:, None] * lam_re
            decay_im = damp[:, None] * lam_im
            projected = jnp.dot(sig, in_weight, preferred_element_type=jnp.float32)
            drive_re = scaling * projected[:, :width]
            drive_im = scaling * projected[:, width:]
            power_re, power_im, local_re, local_im = lax.associative_scan(combine, (decay_re, decay_im, drive_re, drive_im))
            state_re = local_re + power_re * carry[0] - power_im * carry[1]
            state_im = local_im + power_re * carry[1] + power_im * carry[0]
            packed = jnp.concatenate([state_re, state_im], 1).astype(jnp.bfloat16)
            output = lax.dot_general(packed, out_weight, (((1,), (1,)), ((), ())), preferred_element_type=jnp.float32)
            output = (output + skip_gain * sig.astype(jnp.float32)).astype(jnp.bfloat16)
            grad_part = lax.dot_general(upstream, packed, (((0,), (0,)), ((), ())), preferred_element_type=jnp.float32)
            return ((state_re[-1], state_im[-1], carry[2] + grad_part), output)
        start = (jnp.zeros((width,), jnp.float32), jnp.zeros((width,), jnp.float32), totals[1])
        (_, _, acc_out), outputs = lax.scan(forward, start, (sig_blocks, damp_blocks, up_blocks))

        def backward(carry, block):
            sig, damp, upstream = block
            decay_re = damp[:, None] * lam_re
            decay_im = damp[:, None] * lam_im
            grad_packed = jnp.dot(upstream, out_weight, preferred_element_type=jnp.float32)
            shift_re = jnp.concatenate([decay_re[1:], jnp.ones((1, width), jnp.float32)], 0)
            shift_im = jnp.concatenate([-decay_im[1:], jnp.zeros((1, width), jnp.float32)], 0)
            flipped = (jnp.flip(shift_re, 0), jnp.flip(shift_im, 0), jnp.flip(grad_packed[:, :width], 0), jnp.flip(grad_packed[:, width:], 0))
            scanned = lax.associative_scan(combine, flipped)
            back_re, back_im, local_re, local_im = [jnp.flip(item, 0) for item in scanned]
            adj_re = local_re + back_re * carry[0] - back_im * carry[1]
            adj_im = local_im + back_re * carry[1] + back_im * carry[0]
            grad_drive = jnp.concatenate([scaling * adj_re, scaling * adj_im], 1).astype(jnp.bfloat16)
            grad_sig = lax.dot_general(grad_drive, in_weight, (((1,), (1,)), ((), ())), preferred_element_type=jnp.float32)
            grad_sig = (grad_sig + skip_gain * upstream.astype(jnp.float32)).astype(jnp.bfloat16)
            grad_part = lax.dot_general(sig, grad_drive, (((0,), (0,)), ((), ())), preferred_element_type=jnp.float32)
            new_re = decay_re[0] * adj_re[0] + decay_im[0] * adj_im[0]
            new_im = decay_re[0] * adj_im[0] - decay_im[0] * adj_re[0]
            return ((new_re, new_im, carry[2] + grad_part), grad_sig)
        start_back = (jnp.zeros((width,), jnp.float32), jnp.zeros((width,), jnp.float32), totals[0])
        (_, _, acc_in), grads = lax.scan(backward, start_back, (sig_blocks, damp_blocks, up_blocks), reverse=True)
        return ((acc_in, acc_out), (outputs.reshape(TOKEN_STEPS, D), grads.reshape(TOKEN_STEPS, D)))
    zero_grad = jnp.zeros((D, 2 * width), jnp.float32)
    (grad_in, grad_out), (mixed, grad_signal) = lax.scan(record_pass, (zero_grad, zero_grad), (signal, damping, cotangent))
    return (mixed, grad_signal, grad_in, grad_out)
```

```python
import functools

import jax
import jax.numpy as jnp
from jax import lax
from jax.experimental import pallas as pl
from jax.experimental.pallas import tpu as pltpu
from jax.sharding import PartitionSpec as P

MESH = pl.DeviceIdType.MESH
F32 = jnp.float32
BF16 = jnp.bfloat16
SUB = 8
LANE = 128


def cmul(ar, ai, br, bi):
    return ar * br - ai * bi, ar * bi + ai * br


def square_times(re, im, count):
    while count > 1:
        re, im = cmul(re, im, re, im)
        count //= 2
    return re, im


def kernel(
    groups, times,
    sig_ref, damp_ref, par_ref, win_ref, wout_ref, skip_ref, cot_ref,
    mixed_ref, gsig_ref, gin_ref, gout_ref,
    dampb, sigb, cotb, x, y, ends, enters, cmsg, crecv, ldev, cfull,
    fsend, fgat, factor, dsend, dgat, packed, drive, pbuf, zsend, zgat, fsum, osend, ogat,
    csend_sem, crecv_sem, fsend_sem, frecv_sem, dsend_sem, drecv_sem,
    zsend_sem, zrecv_sem, osend_sem, orecv_sem,
):
    steps, feat = sig_ref.shape
    width = par_ref.shape[1]
    inner = steps // SUB
    planes = times // 2
    members = groups * 2
    block = 2 * width // groups
    chunks = block // LANE
    tiles = width // LANE
    own_rows = feat // (groups * times)
    pair_rows = 2 * own_rows

    g = lax.axis_index("grp")
    t = lax.axis_index("tm")
    c = t % 2
    z = t // 2
    me = g * 2 + c

    barrier = pltpu.get_barrier_semaphore()

    def greet_time(d, carry):
        pl.semaphore_signal(barrier, inc=1, device_id=(g, (t + d) % times), device_id_type=MESH)
        return carry

    lax.fori_loop(1, times, greet_time, 0)

    def greet_plane(d, carry):
        pl.semaphore_signal(
            barrier, inc=1, device_id=((g + d // 2) % groups, z * 2 + d % 2), device_id_type=MESH
        )
        return carry

    lax.fori_loop(2, members, greet_plane, 0)

    row = lax.broadcasted_iota(jnp.int32, (steps, steps), 0)
    col = lax.broadcasted_iota(jnp.int32, (steps, steps), 1)
    hit = col == (row % SUB) * inner + row // SUB
    back = row == (col % SUB) * inner + col // SUB
    order = jnp.where(hit, 1.0, 0.0).astype(BF16)
    restore = jnp.where(back, 1.0, 0.0).astype(BF16)
    damp = jnp.sum(jnp.where(hit, damp_ref[...], 0.0), axis=1, keepdims=True)
    dampb[:steps, :] = jnp.broadcast_to(damp, (steps, LANE))
    sig = jnp.dot(order, sig_ref[...], preferred_element_type=F32)
    cot = jnp.dot(order, cot_ref[...], preferred_element_type=F32)
    sigb[...] = sig.astype(BF16)
    cotb[...] = cot.astype(BF16)
    fsend[0] = sig.T
    fsend[1] = cot.T

    pl.semaphore_wait(barrier, (times - 1) + (members - 2))

    def factor_copy(d):
        m = (me + d) % members
        return pltpu.make_async_remote_copy(
            src_ref=fsend.at[m % 2], dst_ref=fgat.at[me],
            send_sem=fsend_sem.at[d], recv_sem=frecv_sem.at[d],
            device_id=(m // 2, z * 2 + m % 2), device_id_type=MESH,
        )

    def start_factor(d, carry):
        factor_copy(d).start()
        return carry

    lax.fori_loop(1, members, start_factor, 0)
    fgat[me] = fsend[c]

    gamma = par_ref[2:3, :]
    x[:, :width] = gamma * jnp.dot(sigb[...], win_ref[:, :width], preferred_element_type=F32)
    x[:, width:] = gamma * jnp.dot(sigb[...], win_ref[:, width:], preferred_element_type=F32)
    y[...] = jnp.dot(cotb[...], wout_ref[...], preferred_element_type=F32)

    lre = jnp.broadcast_to(par_ref[0:1, :], (SUB, width))
    lim = jnp.broadcast_to(par_ref[1:2, :], (SUB, width))

    def rows_of(j):
        return slice(j * SUB, (j + 1) * SUB)

    def forward_step(j, sre, sim):
        rows = rows_of(j)
        a = dampb[rows, 0:1]
        mre, mim = cmul(lre, lim, sre, sim)
        return a * mre + x[rows, :width], a * mim + x[rows, width:]

    def backward_step(j, bre, bim):
        rows = rows_of(j)
        a = dampb[rows, 0:1]
        are = y[rows, :width] + bre
        aim = y[rows, width:] + bim
        return are, aim, a * (lre * are + lim * aim), a * (lre * aim - lim * are)

    zero = jnp.zeros((SUB, width), F32)
    sre, sim = zero, zero
    for j in range(inner):
        sre, sim = forward_step(j, sre, sim)
    ends[0] = sre
    ends[1] = sim
    bre, bim = zero, zero
    for j in reversed(range(inner)):
        _, _, bre, bim = backward_step(j, bre, bim)
    ends[2] = bre
    ends[3] = bim
    prod = dampb[0:SUB, :]
    for j in range(1, inner):
        prod = prod * dampb[rows_of(j), :]
    dampb[steps : steps + SUB, :] = prod

    one_re, one_im = square_times(par_ref[0:1, :], par_ref[1:2, :], inner)
    place = lax.broadcasted_iota(jnp.int32, (SUB, width), 0)

    def edge_power(index):
        pre, pim = jnp.ones((SUB, width), F32), zero
        qre, qim = one_re, one_im
        bit = 1
        while bit < SUB:
            on = (index // bit) % 2 == 1
            pre, pim = cmul(pre, pim, jnp.where(on, qre, 1.0), jnp.where(on, qim, 0.0))
            qre, qim = cmul(qre, qim, qre, qim)
            bit *= 2
        return pre, pim, qre, qim

    pre, pim, dre, dim = edge_power(place)
    tre, tim, _, _ = edge_power(SUB - 1 - place)

    ere = eim = jnp.zeros((1, width), F32)
    total = jnp.ones((1, LANE), F32)
    for o in range(SUB):
        one = slice(o, o + 1)
        enters[0, one] = ere
        enters[1, one] = eim
        dampb[steps + SUB + o : steps + SUB + o + 1, :] = total
        here = dampb[steps + o : steps + o + 1, :]
        mre, mim = cmul(one_re, one_im, ere, eim)
        ere = here[:, 0:1] * mre + ends[0, one]
        eim = here[:, 0:1] * mim + ends[1, one]
        total = total * here
    ore = oim = jnp.zeros((1, width), F32)
    tail = jnp.ones((1, LANE), F32)
    for o in reversed(range(SUB)):
        one = slice(o, o + 1)
        enters[2, one] = ore
        enters[3, one] = oim
        dampb[steps + 2 * SUB + o : steps + 2 * SUB + o + 1, :] = tail
        here = dampb[steps + o : steps + o + 1, :]
        mre = one_re * ore + one_im * oim
        mim = one_re * oim - one_im * ore
        ore = here[:, 0:1] * mre + ends[2, one]
        oim = here[:, 0:1] * mim + ends[3, one]
        tail = tail * here

    for i in range(tiles):
        lanes = slice(i * LANE, (i + 1) * LANE)
        one = slice(i, i + 1)
        cmsg[0, 0, one] = ere[:, lanes]
        cmsg[0, 1, one] = eim[:, lanes]
        cmsg[1, 0, one] = ore[:, lanes]
        cmsg[1, 1, one] = oim[:, lanes]
        ldev[0, one] = dre[:, lanes]
        ldev[1, one] = dim[:, lanes]
    cmsg[0, 2] = jnp.broadcast_to(total, (tiles, LANE))
    cmsg[1, 2] = jnp.broadcast_to(total, (tiles, LANE))

    def carry_copy(q):
        later = jnp.where(q > t, 0, 1)
        return pltpu.make_async_remote_copy(
            src_ref=cmsg.at[later], dst_ref=crecv.at[t],
            send_sem=csend_sem.at[q], recv_sem=crecv_sem.at[t],
            device_id=(g, q), device_id_type=MESH,
        )

    def carry_arrival(q):
        return pltpu.make_async_remote_copy(
            src_ref=cmsg.at[0], dst_ref=crecv.at[q],
            send_sem=csend_sem.at[q], recv_sem=crecv_sem.at[q],
            device_id=(g, q), device_id_type=MESH,
        )

    def start_carry(d, carry):
        carry_copy((t + d) % times).start()
        return carry

    lax.fori_loop(1, times, start_carry, 0)

    def ahead(q, carry):
        carry_arrival(q).wait_recv()
        mre, mim = cmul(ldev[0], ldev[1], carry[0], carry[1])
        factor_q = crecv[q, 2]
        return factor_q * mre + crecv[q, 0], factor_q * mim + crecv[q, 1]

    def behind(i, carry):
        q = times - 1 - i
        carry_arrival(q).wait_recv()
        mre = ldev[0] * carry[0] + ldev[1] * carry[1]
        mim = ldev[0] * carry[1] - ldev[1] * carry[0]
        factor_q = crecv[q, 2]
        return factor_q * mre + crecv[q, 0], factor_q * mim + crecv[q, 1]

    none = jnp.zeros((tiles, LANE), F32)
    cfull[0], cfull[1] = lax.fori_loop(0, t, ahead, (none, none))
    cfull[2], cfull[3] = lax.fori_loop(0, times - 1 - t, behind, (none, none))

    def wide(i):
        return jnp.concatenate([cfull[i, k : k + 1, :] for k in range(tiles)], axis=1)

    def rounded(value):
        return value.astype(BF16).astype(F32)

    mre, mim = cmul(pre, pim, wide(0), wide(1))
    reach = dampb[steps + SUB : steps + 2 * SUB, 0:1]
    sre = enters[0] + reach * mre
    sim = enters[1] + reach * mim
    for j in range(inner):
        sre, sim = forward_step(j, sre, sim)
        kre, kim = rounded(sre), rounded(sim)
        for i in range(tiles):
            lanes = slice(i * LANE, (i + 1) * LANE)
            dsend[1, i, rows_of(j)] = kre[:, lanes]
            dsend[1, tiles + i, rows_of(j)] = kim[:, lanes]

    kre, kim = wide(2), wide(3)
    mre = tre * kre + tim * kim
    mim = tre * kim - tim * kre
    reach = dampb[steps + 2 * SUB : steps + 3 * SUB, 0:1]
    bre = enters[2] + reach * mre
    bim = enters[3] + reach * mim
    for j in reversed(range(inner)):
        are, aim, bre, bim = backward_step(j, bre, bim)
        kre, kim = rounded(gamma * are), rounded(gamma * aim)
        for i in range(tiles):
            lanes = slice(i * LANE, (i + 1) * LANE)
            dsend[0, i, rows_of(j)] = kre[:, lanes]
            dsend[0, tiles + i, rows_of(j)] = kim[:, lanes]

    def drive_copy(k, d):
        m = (me + d) % members
        return pltpu.make_async_remote_copy(
            src_ref=dsend.at[m % 2, (m // 2) * chunks + k], dst_ref=dgat.at[k, me],
            send_sem=dsend_sem.at[k, d], recv_sem=drecv_sem.at[k, d],
            device_id=(m // 2, z * 2 + m % 2), device_id_type=MESH,
        )

    for k in range(chunks):
        def start_drive(d, carry, k=k):
            drive_copy(k, d).start()
            return carry

        lax.fori_loop(1, members, start_drive, 0)

    for k in range(chunks):
        dgat[k, me] = dsend[c, g * chunks + k]

    for i in range(2 * tiles):
        lanes = slice(i * LANE, (i + 1) * LANE)
        packed[:, lanes] = dsend[1, i].astype(BF16)
        drive[:, lanes] = dsend[0, i].astype(BF16)

    turned = (((1,), (1,)), ((), ()))
    out = lax.dot_general(packed[...], wout_ref[...], turned, preferred_element_type=F32)
    out = (out + skip_ref[...] * sigb[...].astype(F32)).astype(BF16)
    mixed_ref[...] = jnp.dot(restore, out, preferred_element_type=F32).astype(BF16)
    out = lax.dot_general(drive[...], win_ref[...], turned, preferred_element_type=F32)
    out = (out + skip_ref[...] * cotb[...].astype(F32)).astype(BF16)
    gsig_ref[...] = jnp.dot(restore, out, preferred_element_type=F32).astype(BF16)

    def await_factor(d, carry):
        factor_copy(d).wait_recv()
        return carry

    lax.fori_loop(1, members, await_factor, 0)
    for m in range(members):
        factor[:, m * steps : (m + 1) * steps] = fgat[m].astype(BF16)

    def plane_copy(k, d):
        other = (z + d) % planes
        return pltpu.make_async_remote_copy(
            src_ref=zsend.at[k, other], dst_ref=zgat.at[k, z],
            send_sem=zsend_sem.at[k, d], recv_sem=zrecv_sem.at[k, d],
            device_id=(g, other * 2 + c), device_id_type=MESH,
        )

    for k in range(chunks):
        def await_drive(d, carry, k=k):
            drive_copy(k, d).wait_recv()
            return carry

        lax.fori_loop(1, members, await_drive, 0)
        whole = dgat[k].reshape(members * steps, LANE).astype(BF16)
        pbuf[k] = jnp.dot(factor[...], whole, preferred_element_type=F32)
        for gg in range(groups):
            for zz in range(planes):
                first = gg * times * own_rows + zz * pair_rows
                zsend[k, zz, gg * pair_rows : (gg + 1) * pair_rows] = pbuf[k, first : first + pair_rows]

        def start_plane(d, carry, k=k):
            plane_copy(k, d).start()
            return carry

        lax.fori_loop(1, planes, start_plane, 0)

    for k in range(chunks):
        def add_plane(d, acc, k=k):
            plane_copy(k, d).wait_recv()
            return acc + zgat[k, (z + planes - d) % planes]

        fsum[:, k * LANE : (k + 1) * LANE] = lax.fori_loop(1, planes, add_plane, zsend[k, z])

    for m in range(members):
        osend[m] = fsum[m * own_rows : (m + 1) * own_rows, :]

    def owner_copy(d):
        m = (me + d) % members
        return pltpu.make_async_remote_copy(
            src_ref=osend.at[m], dst_ref=ogat.at[me],
            send_sem=osend_sem.at[d], recv_sem=orecv_sem.at[d],
            device_id=(m // 2, z * 2 + m % 2), device_id_type=MESH,
        )

    def start_owner(d, carry):
        owner_copy(d).start()
        return carry

    lax.fori_loop(1, members, start_owner, 0)
    ogat[me] = osend[me]

    def await_owner(d, carry):
        owner_copy(d).wait_recv()
        return carry

    lax.fori_loop(1, members, await_owner, 0)
    for gg in range(groups):
        lanes = slice(gg * block, (gg + 1) * block)
        gin_ref[:, lanes] = ogat[gg * 2]
        gout_ref[:, lanes] = ogat[gg * 2 + 1]

    def drain_members(d, carry):
        factor_copy(d).wait_send()
        owner_copy(d).wait_send()
        for k in range(chunks):
            drive_copy(k, d).wait_send()
        return carry

    lax.fori_loop(1, members, drain_members, 0)

    def drain_planes(d, carry):
        for k in range(chunks):
            plane_copy(k, d).wait_send()
        return carry

    lax.fori_loop(1, planes, drain_planes, 0)

    def drain_times(d, carry):
        carry_copy((t + d) % times).wait_send()
        return carry

    lax.fori_loop(1, times, drain_times, 0)


def body(groups, times, signal, damping, nu_log, theta, in_weight, out_weight, skip_gain, cotangent):
    _, steps, feat = signal.shape
    width = nu_log.shape[0]
    rate = jnp.exp(nu_log)
    magnitude = jnp.exp(-rate)
    scaling = jnp.sqrt(-jnp.expm1(-2.0 * rate))
    par = jnp.stack([magnitude * jnp.cos(theta), magnitude * jnp.sin(theta), scaling], 0)
    members = groups * 2
    planes = times // 2
    block = 2 * width // groups
    chunks = block // LANE
    tiles = width // LANE
    own_rows = feat // (groups * times)
    plane_rows = feat // planes
    vmem = pl.BlockSpec(memory_space=pltpu.VMEM)
    dma = pltpu.SemaphoreType.DMA
    scratch = [
        pltpu.VMEM((steps + 3 * SUB, LANE), F32),
        pltpu.VMEM((steps, feat), BF16),
        pltpu.VMEM((steps, feat), BF16),
        pltpu.VMEM((steps, 2 * width), F32),
        pltpu.VMEM((steps, 2 * width), F32),
        pltpu.VMEM((4, SUB, width), F32),
        pltpu.VMEM((4, SUB, width), F32),
        pltpu.VMEM((2, 3, tiles, LANE), F32),
        pltpu.VMEM((times, 3, tiles, LANE), F32),
        pltpu.VMEM((2, tiles, LANE), F32),
        pltpu.VMEM((4, tiles, LANE), F32),
        pltpu.VMEM((2, feat, steps), F32),
        pltpu.VMEM((members, feat, steps), F32),
        pltpu.VMEM((feat, members * steps), BF16),
        pltpu.VMEM((2, 2 * tiles, steps, LANE), F32),
        pltpu.VMEM((chunks, members, steps, LANE), F32),
        pltpu.VMEM((steps, 2 * width), BF16),
        pltpu.VMEM((steps, 2 * width), BF16),
        pltpu.VMEM((chunks, feat, LANE), F32),
        pltpu.VMEM((chunks, planes, plane_rows, LANE), F32),
        pltpu.VMEM((chunks, planes, plane_rows, LANE), F32),
        pltpu.VMEM((plane_rows, block), F32),
        pltpu.VMEM((members, own_rows, block), F32),
        pltpu.VMEM((members, own_rows, block), F32),
        dma((times,)), dma((times,)),
        dma((members,)), dma((members,)),
        dma((chunks, members)), dma((chunks, members)),
        dma((chunks, planes)), dma((chunks, planes)),
        dma((members,)), dma((members,)),
    ]
    out = pl.pallas_call(
        functools.partial(kernel, groups, times),
        out_shape=(
            jax.ShapeDtypeStruct((steps, feat), BF16),
            jax.ShapeDtypeStruct((steps, feat), BF16),
            jax.ShapeDtypeStruct((own_rows, 2 * width), F32),
            jax.ShapeDtypeStruct((own_rows, 2 * width), F32),
        ),
        in_specs=[vmem] * 7,
        out_specs=(vmem,) * 4,
        scratch_shapes=scratch,
        compiler_params=pltpu.CompilerParams(
            collective_id=0, has_side_effects=True, vmem_limit_bytes=48 * 1024 * 1024
        ),
        cost_estimate=pl.CostEstimate(
            flops=14 * steps * feat * 2 * width, bytes_accessed=8 * feat * width, transcendentals=0
        ),
    )(signal[0], damping, par, in_weight, out_weight, skip_gain[None], cotangent[0])
    return (out[0][None], out[1][None], out[2], out[3])


def solution(mesh):
    placed = (P("grp", "tm", None), P("grp", "tm"), P(), P(), P(), P(), P(), P("grp", "tm", None))
    return jax.shard_map(
        functools.partial(body, mesh.shape["grp"], mesh.shape["tm"]),
        mesh=mesh,
        in_specs=placed,
        out_specs=(
            P("grp", "tm", None),
            P("grp", "tm", None),
            P(("grp", "tm"), None),
            P(("grp", "tm"), None),
        ),
        check_vma=False,
    )
```

```python
import functools

import jax
import jax.numpy as jnp
from jax import lax
from jax.experimental import pallas as pl
from jax.experimental.pallas import tpu as pltpu
from jax.sharding import PartitionSpec as P

MESH = pl.DeviceIdType.MESH
F32 = jnp.float32
BF16 = jnp.bfloat16
SUB = 8
LANE = 128


def cmul(ar, ai, br, bi):
    return ar * br - ai * bi, ar * bi + ai * br


def square_times(re, im, count):
    while count > 1:
        re, im = cmul(re, im, re, im)
        count //= 2
    return re, im


def kernel(
    groups, times,
    sig_hbm, damp_hbm, par_ref, win_hbm, wout_hbm, skip_hbm, cot_hbm,
    mixed_ref, gsig_ref, gin_ref, gout_ref,
    sig_ref, damp_ref, win_ref, wout_ref, skip_ref, cot_ref, load_sem,
    dampb, sigb, cotb, x, y, ends, enters, cmsg, crecv, ldev, cfull,
    fsend, fgat, factor, dsend, dgat, packed, drive, pbuf, rsend, rgat, zsend, zgat, osend, ogat,
    csend_sem, crecv_sem, fsend_sem, frecv_sem, dsend_sem, drecv_sem,
    rsend_sem, rrecv_sem, zsend_sem, zrecv_sem, osend_sem, orecv_sem,
):
    steps, feat = sig_hbm.shape
    width = par_ref.shape[1]
    inner = steps // SUB
    planes = times // 2
    members = groups * 2
    block = 2 * width // groups
    chunks = block // LANE
    tiles = width // LANE
    own_rows = feat // (groups * times)
    pair_rows = 2 * own_rows
    units = 2 * chunks

    g = lax.axis_index("grp")
    t = lax.axis_index("tm")
    c = t % 2
    z = t // 2
    me = g * 2 + c

    hi = g // 2
    lo = g % 2

    loads = [
        pltpu.make_async_copy(src, dst, load_sem.at[i])
        for i, (src, dst) in enumerate(
            (
                (sig_hbm, sig_ref), (cot_hbm, cot_ref), (damp_hbm, damp_ref),
                (win_hbm, win_ref), (wout_hbm, wout_ref), (skip_hbm, skip_ref),
            )
        )
    ]
    for load in loads:
        load.start()

    barrier = pltpu.get_barrier_semaphore()

    def greet_time(d, carry):
        pl.semaphore_signal(barrier, inc=1, device_id=(g, (t + d) % times), device_id_type=MESH)
        return carry

    lax.fori_loop(1, times, greet_time, 0)

    def greet_plane(d, carry):
        pl.semaphore_signal(
            barrier, inc=1, device_id=((g + d // 2) % groups, z * 2 + d % 2), device_id_type=MESH
        )
        return carry

    lax.fori_loop(2, members, greet_plane, 0)

    for load in loads[:3]:
        load.wait()

    row = lax.broadcasted_iota(jnp.int32, (steps, steps), 0)
    col = lax.broadcasted_iota(jnp.int32, (steps, steps), 1)
    hit = col == (row % SUB) * inner + row // SUB
    back = row == (col % SUB) * inner + col // SUB
    order = jnp.where(hit, 1.0, 0.0).astype(BF16)
    restore = jnp.where(back, 1.0, 0.0).astype(BF16)
    damp = jnp.sum(jnp.where(hit, damp_ref[...], 0.0), axis=1, keepdims=True)
    dampb[:steps, :] = jnp.broadcast_to(damp, (steps, LANE))
    sig = jnp.dot(order, sig_ref[...], preferred_element_type=F32)
    cot = jnp.dot(order, cot_ref[...], preferred_element_type=F32)
    sigb[...] = sig.astype(BF16)
    cotb[...] = cot.astype(BF16)
    fsend[0] = sig.T
    fsend[1] = cot.T

    pl.semaphore_wait(barrier, (times - 1) + (members - 2))

    def place_of(kind):
        return jnp.where(kind == 0, lo, hi)

    def flipped(device, kind):
        return jnp.where(kind == 0, (device + 2) % groups, device + 1 - 2 * (device % 2))

    def pair_target(d):
        kind = c if d == 0 else 1 - c
        mine = place_of(kind)
        theirs = mine if d == 1 else 1 - mine
        device = jnp.where(kind == 0, hi * 2 + theirs, theirs * 2 + lo)
        return kind, device, mine * 2 + c

    def factor_copy(d):
        kind, device, slot = pair_target(d)
        return pltpu.make_async_remote_copy(
            src_ref=fsend.at[kind], dst_ref=fgat.at[slot],
            send_sem=fsend_sem.at[d], recv_sem=frecv_sem.at[d],
            device_id=(device, z * 2 + kind), device_id_type=MESH,
        )

    for d in (0, 2, 1):
        factor_copy(d).start()
    own_slot = place_of(c) * 2 + c
    fgat[own_slot] = fsend[c]

    for load in loads[3:]:
        load.wait()
    gamma = par_ref[2:3, :]
    x[:, :width] = gamma * jnp.dot(sigb[...], win_ref[:, :width], preferred_element_type=F32)
    x[:, width:] = gamma * jnp.dot(sigb[...], win_ref[:, width:], preferred_element_type=F32)
    y[...] = jnp.dot(cotb[...], wout_ref[...], preferred_element_type=F32)

    lre = jnp.broadcast_to(par_ref[0:1, :], (SUB, width))
    lim = jnp.broadcast_to(par_ref[1:2, :], (SUB, width))

    def rows_of(j):
        return slice(j * SUB, (j + 1) * SUB)

    def forward_step(j, sre, sim):
        rows = rows_of(j)
        a = dampb[rows, 0:1]
        mre, mim = cmul(lre, lim, sre, sim)
        return a * mre + x[rows, :width], a * mim + x[rows, width:]

    def backward_step(j, bre, bim):
        rows = rows_of(j)
        a = dampb[rows, 0:1]
        are = y[rows, :width] + bre
        aim = y[rows, width:] + bim
        return are, aim, a * (lre * are + lim * aim), a * (lre * aim - lim * are)

    zero = jnp.zeros((SUB, width), F32)
    sre, sim = zero, zero
    for j in range(inner):
        sre, sim = forward_step(j, sre, sim)
    ends[0] = sre
    ends[1] = sim
    bre, bim = zero, zero
    for j in reversed(range(inner)):
        _, _, bre, bim = backward_step(j, bre, bim)
    ends[2] = bre
    ends[3] = bim
    prod = dampb[0:SUB, :]
    for j in range(1, inner):
        prod = prod * dampb[rows_of(j), :]
    dampb[steps : steps + SUB, :] = prod

    one_re, one_im = square_times(par_ref[0:1, :], par_ref[1:2, :], inner)
    place = lax.broadcasted_iota(jnp.int32, (SUB, width), 0)

    def edge_power(index):
        pre, pim = jnp.ones((SUB, width), F32), zero
        qre, qim = one_re, one_im
        bit = 1
        while bit < SUB:
            on = (index // bit) % 2 == 1
            pre, pim = cmul(pre, pim, jnp.where(on, qre, 1.0), jnp.where(on, qim, 0.0))
            qre, qim = cmul(qre, qim, qre, qim)
            bit *= 2
        return pre, pim, qre, qim

    pre, pim, dre, dim = edge_power(place)
    tre, tim, _, _ = edge_power(SUB - 1 - place)

    ere = eim = jnp.zeros((1, width), F32)
    total = jnp.ones((1, LANE), F32)
    for o in range(SUB):
        one = slice(o, o + 1)
        enters[0, one] = ere
        enters[1, one] = eim
        dampb[steps + SUB + o : steps + SUB + o + 1, :] = total
        here = dampb[steps + o : steps + o + 1, :]
        mre, mim = cmul(one_re, one_im, ere, eim)
        ere = here[:, 0:1] * mre + ends[0, one]
        eim = here[:, 0:1] * mim + ends[1, one]
        total = total * here
    ore = oim = jnp.zeros((1, width), F32)
    tail = jnp.ones((1, LANE), F32)
    for o in reversed(range(SUB)):
        one = slice(o, o + 1)
        enters[2, one] = ore
        enters[3, one] = oim
        dampb[steps + 2 * SUB + o : steps + 2 * SUB + o + 1, :] = tail
        here = dampb[steps + o : steps + o + 1, :]
        mre = one_re * ore + one_im * oim
        mim = one_re * oim - one_im * ore
        ore = here[:, 0:1] * mre + ends[2, one]
        oim = here[:, 0:1] * mim + ends[3, one]
        tail = tail * here

    for i in range(tiles):
        lanes = slice(i * LANE, (i + 1) * LANE)
        one = slice(i, i + 1)
        cmsg[0, 0, one] = ere[:, lanes]
        cmsg[0, 1, one] = eim[:, lanes]
        cmsg[1, 0, one] = ore[:, lanes]
        cmsg[1, 1, one] = oim[:, lanes]
        ldev[0, one] = dre[:, lanes]
        ldev[1, one] = dim[:, lanes]
    cmsg[0, 2] = jnp.broadcast_to(total, (tiles, LANE))
    cmsg[1, 2] = jnp.broadcast_to(total, (tiles, LANE))

    def carry_copy(q):
        later = jnp.where(q > t, 0, 1)
        return pltpu.make_async_remote_copy(
            src_ref=cmsg.at[later], dst_ref=crecv.at[t],
            send_sem=csend_sem.at[q], recv_sem=crecv_sem.at[t],
            device_id=(g, q), device_id_type=MESH,
        )

    def carry_arrival(q):
        return pltpu.make_async_remote_copy(
            src_ref=cmsg.at[0], dst_ref=crecv.at[q],
            send_sem=csend_sem.at[q], recv_sem=crecv_sem.at[q],
            device_id=(g, q), device_id_type=MESH,
        )

    def start_carry(d, carry):
        carry_copy((t + d) % times).start()
        return carry

    lax.fori_loop(1, times, start_carry, 0)

    def ahead(q, carry):
        carry_arrival(q).wait_recv()
        mre, mim = cmul(ldev[0], ldev[1], carry[0], carry[1])
        factor_q = crecv[q, 2]
        return factor_q * mre + crecv[q, 0], factor_q * mim + crecv[q, 1]

    def behind(i, carry):
        q = times - 1 - i
        carry_arrival(q).wait_recv()
        mre = ldev[0] * carry[0] + ldev[1] * carry[1]
        mim = ldev[0] * carry[1] - ldev[1] * carry[0]
        factor_q = crecv[q, 2]
        return factor_q * mre + crecv[q, 0], factor_q * mim + crecv[q, 1]

    none = jnp.zeros((tiles, LANE), F32)
    cfull[0], cfull[1] = lax.fori_loop(0, t, ahead, (none, none))
    cfull[2], cfull[3] = lax.fori_loop(0, times - 1 - t, behind, (none, none))

    def wide(i):
        return jnp.concatenate([cfull[i, k : k + 1, :] for k in range(tiles)], axis=1)

    def rounded(value):
        return value.astype(BF16).astype(F32)

    mre, mim = cmul(pre, pim, wide(0), wide(1))
    reach = dampb[steps + SUB : steps + 2 * SUB, 0:1]
    sre = enters[0] + reach * mre
    sim = enters[1] + reach * mim
    for j in range(inner):
        sre, sim = forward_step(j, sre, sim)
        kre, kim = rounded(sre), rounded(sim)
        for i in range(tiles):
            lanes = slice(i * LANE, (i + 1) * LANE)
            dsend[1, i, rows_of(j)] = kre[:, lanes]
            dsend[1, tiles + i, rows_of(j)] = kim[:, lanes]

    def unit_column(u, device, kind):
        keeper = device if u % 2 else flipped(device, kind)
        return keeper * chunks + u // 2

    def drive_copy(u, d):
        kind, device, slot = pair_target(d)
        return pltpu.make_async_remote_copy(
            src_ref=dsend.at[kind, unit_column(u, device, kind)], dst_ref=dgat.at[u, slot],
            send_sem=dsend_sem.at[u, d], recv_sem=drecv_sem.at[u, d],
            device_id=(device, z * 2 + kind), device_id_type=MESH,
        )

    def start_drive(kind):
        @pl.when(c == kind)
        def _():
            for u in range(units):
                drive_copy(u, 0).start()

        @pl.when(c != kind)
        def _():
            for u in range(units):
                drive_copy(u, 2).start()
                drive_copy(u, 1).start()

    start_drive(1)

    kre, kim = wide(2), wide(3)
    mre = tre * kre + tim * kim
    mim = tre * kim - tim * kre
    reach = dampb[steps + 2 * SUB : steps + 3 * SUB, 0:1]
    bre = enters[2] + reach * mre
    bim = enters[3] + reach * mim
    for j in reversed(range(inner)):
        are, aim, bre, bim = backward_step(j, bre, bim)
        kre, kim = rounded(gamma * are), rounded(gamma * aim)
        for i in range(tiles):
            lanes = slice(i * LANE, (i + 1) * LANE)
            dsend[0, i, rows_of(j)] = kre[:, lanes]
            dsend[0, tiles + i, rows_of(j)] = kim[:, lanes]

    start_drive(0)
    for u in range(units):
        dgat[u, own_slot] = dsend[c, unit_column(u, g, c)]

    for i in range(2 * tiles):
        lanes = slice(i * LANE, (i + 1) * LANE)
        packed[:, lanes] = dsend[1, i].astype(BF16)
        drive[:, lanes] = dsend[0, i].astype(BF16)

    turned = (((1,), (1,)), ((), ()))
    out = lax.dot_general(packed[...], wout_ref[...], turned, preferred_element_type=F32)
    out = (out + skip_ref[...] * sigb[...].astype(F32)).astype(BF16)
    mixed_ref[...] = jnp.dot(restore, out, preferred_element_type=F32).astype(BF16)
    out = lax.dot_general(drive[...], win_ref[...], turned, preferred_element_type=F32)
    out = (out + skip_ref[...] * cotb[...].astype(F32)).astype(BF16)
    gsig_ref[...] = jnp.dot(restore, out, preferred_element_type=F32).astype(BF16)

    for d in range(3):
        factor_copy(d).wait_recv()
    for m in range(4):
        factor[:, m * steps : (m + 1) * steps] = fgat[m].astype(BF16)

    def partner_copy(k):
        return pltpu.make_async_remote_copy(
            src_ref=rsend.at[k], dst_ref=rgat.at[k],
            send_sem=rsend_sem.at[k], recv_sem=rrecv_sem.at[k],
            device_id=(flipped(g, c), t), device_id_type=MESH,
        )

    def plane_copy(k, d):
        other = (z + d) % planes
        return pltpu.make_async_remote_copy(
            src_ref=zsend.at[k, other], dst_ref=zgat.at[k, z],
            send_sem=zsend_sem.at[k, d], recv_sem=zrecv_sem.at[k, d],
            device_id=(g, other * 2 + c), device_id_type=MESH,
        )

    def owner_copy(k, d):
        m = (me + d) % members
        return pltpu.make_async_remote_copy(
            src_ref=osend.at[k, m], dst_ref=ogat.at[k, me],
            send_sem=osend_sem.at[k, d], recv_sem=orecv_sem.at[k, d],
            device_id=(m // 2, z * 2 + m % 2), device_id_type=MESH,
        )

    def product(u):
        for d in range(3):
            drive_copy(u, d).wait_recv()
        whole = dgat[u].reshape(4 * steps, LANE).astype(BF16)
        return jnp.dot(factor[...], whole, preferred_element_type=F32)

    def multiply(k):
        rsend[k] = product(2 * k)
        partner_copy(k).start()
        pbuf[k] = product(2 * k + 1)

    def add_partner(k):
        partner_copy(k).wait_recv()
        for gg in range(groups):
            for zz in range(planes):
                first = gg * times * own_rows + zz * pair_rows
                rows = slice(first, first + pair_rows)
                zsend[k, zz, gg * pair_rows : (gg + 1) * pair_rows] = pbuf[k, rows] + rgat[k, rows]

        def start_plane(d, carry):
            plane_copy(k, d).start()
            return carry

        lax.fori_loop(1, planes, start_plane, 0)

    def add_planes(k):
        def add_plane(d, acc):
            plane_copy(k, d).wait_recv()
            return acc + zgat[k, (z + planes - d) % planes]

        pbuf[k, : members * own_rows] = lax.fori_loop(1, planes, add_plane, zsend[k, z])
        for m in range(members):
            osend[k, m] = pbuf[k, m * own_rows : (m + 1) * own_rows]

        def start_owner(d, carry):
            owner_copy(k, d).start()
            return carry

        lax.fori_loop(1, members, start_owner, 0)
        ogat[k, me] = osend[k, me]

    def finish(k):
        def await_owner(d, carry):
            owner_copy(k, d).wait_recv()
            return carry

        lax.fori_loop(1, members, await_owner, 0)
        for gg in range(groups):
            lanes = slice((gg * chunks + k) * LANE, (gg * chunks + k + 1) * LANE)
            gin_ref[:, lanes] = ogat[k, gg * 2]
            gout_ref[:, lanes] = ogat[k, gg * 2 + 1]

    for s in range(chunks + 4):
        if s < chunks:
            multiply(s)
        if 0 <= s - 1 < chunks:
            add_partner(s - 1)
        if 0 <= s - 3 < chunks:
            add_planes(s - 3)
        if 0 <= s - 4 < chunks:
            finish(s - 4)

    for d in range(3):
        factor_copy(d).wait_send()
        for u in range(units):
            drive_copy(u, d).wait_send()
    for k in range(chunks):
        partner_copy(k).wait_send()

    def drain_members(d, carry):
        for k in range(chunks):
            owner_copy(k, d).wait_send()
        return carry

    lax.fori_loop(1, members, drain_members, 0)

    def drain_planes(d, carry):
        for k in range(chunks):
            plane_copy(k, d).wait_send()
        return carry

    lax.fori_loop(1, planes, drain_planes, 0)

    def drain_times(d, carry):
        carry_copy((t + d) % times).wait_send()
        return carry

    lax.fori_loop(1, times, drain_times, 0)


def body(groups, times, signal, damping, nu_log, theta, in_weight, out_weight, skip_gain, cotangent):
    _, steps, feat = signal.shape
    width = nu_log.shape[0]
    rate = jnp.exp(nu_log)
    magnitude = jnp.exp(-rate)
    scaling = jnp.sqrt(-jnp.expm1(-2.0 * rate))
    par = jnp.stack([magnitude * jnp.cos(theta), magnitude * jnp.sin(theta), scaling], 0)
    members = groups * 2
    planes = times // 2
    block = 2 * width // groups
    chunks = block // LANE
    tiles = width // LANE
    own_rows = feat // (groups * times)
    plane_rows = feat // planes
    vmem = pl.BlockSpec(memory_space=pltpu.VMEM)
    dma = pltpu.SemaphoreType.DMA
    scratch = [
        pltpu.VMEM((steps, feat), BF16),
        pltpu.VMEM((1, steps), F32),
        pltpu.VMEM((feat, 2 * width), BF16),
        pltpu.VMEM((feat, 2 * width), BF16),
        pltpu.VMEM((1, feat), F32),
        pltpu.VMEM((steps, feat), BF16),
        dma((6,)),
        pltpu.VMEM((steps + 3 * SUB, LANE), F32),
        pltpu.VMEM((steps, feat), BF16),
        pltpu.VMEM((steps, feat), BF16),
        pltpu.VMEM((steps, 2 * width), F32),
        pltpu.VMEM((steps, 2 * width), F32),
        pltpu.VMEM((4, SUB, width), F32),
        pltpu.VMEM((4, SUB, width), F32),
        pltpu.VMEM((2, 3, tiles, LANE), F32),
        pltpu.VMEM((times, 3, tiles, LANE), F32),
        pltpu.VMEM((2, tiles, LANE), F32),
        pltpu.VMEM((4, tiles, LANE), F32),
        pltpu.VMEM((2, feat, steps), F32),
        pltpu.VMEM((4, feat, steps), F32),
        pltpu.VMEM((feat, 4 * steps), BF16),
        pltpu.VMEM((2, 2 * tiles, steps, LANE), F32),
        pltpu.VMEM((2 * chunks, 4, steps, LANE), F32),
        pltpu.VMEM((steps, 2 * width), BF16),
        pltpu.VMEM((steps, 2 * width), BF16),
        pltpu.VMEM((chunks, feat, LANE), F32),
        pltpu.VMEM((chunks, feat, LANE), F32),
        pltpu.VMEM((chunks, feat, LANE), F32),
        pltpu.VMEM((chunks, planes, plane_rows, LANE), F32),
        pltpu.VMEM((chunks, planes, plane_rows, LANE), F32),
        pltpu.VMEM((chunks, members, own_rows, LANE), F32),
        pltpu.VMEM((chunks, members, own_rows, LANE), F32),
        dma((times,)), dma((times,)),
        dma((3,)), dma((3,)),
        dma((2 * chunks, 3)), dma((2 * chunks, 3)),
        dma((chunks,)), dma((chunks,)),
        dma((chunks, planes)), dma((chunks, planes)),
        dma((chunks, members)), dma((chunks, members)),
    ]
    hbm = pl.BlockSpec(memory_space=pl.ANY)
    out = pl.pallas_call(
        functools.partial(kernel, groups, times),
        out_shape=(
            jax.ShapeDtypeStruct((steps, feat), BF16),
            jax.ShapeDtypeStruct((steps, feat), BF16),
            jax.ShapeDtypeStruct((own_rows, 2 * width), F32),
            jax.ShapeDtypeStruct((own_rows, 2 * width), F32),
        ),
        in_specs=[hbm, hbm, vmem, hbm, hbm, hbm, hbm],
        out_specs=(vmem,) * 4,
        scratch_shapes=scratch,
        compiler_params=pltpu.CompilerParams(
            collective_id=0, has_side_effects=True, vmem_limit_bytes=48 * 1024 * 1024
        ),
        cost_estimate=pl.CostEstimate(
            flops=14 * steps * feat * 2 * width, bytes_accessed=8 * feat * width, transcendentals=0
        ),
    )(signal[0], damping, par, in_weight, out_weight, skip_gain[None], cotangent[0])
    return (out[0][None], out[1][None], out[2], out[3])


def solution(mesh):
    placed = (P("grp", "tm", None), P("grp", "tm"), P(), P(), P(), P(), P(), P("grp", "tm", None))
    return jax.shard_map(
        functools.partial(body, mesh.shape["grp"], mesh.shape["tm"]),
        mesh=mesh,
        in_specs=placed,
        out_specs=(
            P("grp", "tm", None),
            P("grp", "tm", None),
            P(("grp", "tm"), None),
            P(("grp", "tm"), None),
        ),
        check_vma=False,
    )
```

```python
import functools

import jax
import jax.numpy as jnp
from jax import lax
from jax.experimental import pallas as pl
from jax.experimental.pallas import tpu as pltpu
from jax.sharding import PartitionSpec as P

MESH = pl.DeviceIdType.MESH
F32 = jnp.float32
BF16 = jnp.bfloat16
SUB = 8
LANE = 128


def cmul(ar, ai, br, bi):
    return ar * br - ai * bi, ar * bi + ai * br


def square_times(re, im, count):
    while count > 1:
        re, im = cmul(re, im, re, im)
        count //= 2
    return re, im


def kernel(
    groups, times,
    sig_hbm, damp_hbm, par_ref, win_hbm, wout_hbm, skip_hbm, cot_hbm,
    mixed_ref, gsig_ref, gin_ref, gout_ref,
    sig_ref, damp_ref, win_ref, wout_ref, skip_ref, cot_ref, load_sem,
    dampb, sigb, cotb, x, y, ends, enters, cmsg, crecv, ldev, cfull,
    fsend, fgat, factor, dsend, dgat, packed, drive, pbuf, rsend, rgat, zsend, zgat, osend, ogat,
    csend_sem, crecv_sem, fsend_sem, frecv_sem, dsend_sem, drecv_sem,
    rsend_sem, rrecv_sem, zsend_sem, zrecv_sem, osend_sem, orecv_sem,
):
    steps, feat = sig_hbm.shape
    width = par_ref.shape[1]
    inner = steps // SUB
    planes = times // 2
    members = groups * 2
    block = 2 * width // groups
    chunks = block // LANE
    tiles = width // LANE
    own_rows = feat // (groups * times)
    pair_rows = 2 * own_rows
    units = 2 * chunks

    g = lax.axis_index("grp")
    t = lax.axis_index("tm")
    c = t % 2
    z = t // 2
    me = g * 2 + c

    hi = g // 2
    lo = g % 2

    loads = [
        pltpu.make_async_copy(src, dst, load_sem.at[i])
        for i, (src, dst) in enumerate(
            (
                (sig_hbm, sig_ref), (cot_hbm, cot_ref), (damp_hbm, damp_ref),
                (win_hbm, win_ref), (wout_hbm, wout_ref), (skip_hbm, skip_ref),
            )
        )
    ]
    for load in loads:
        load.start()

    barrier = pltpu.get_barrier_semaphore()

    def greet_time(d, carry):
        pl.semaphore_signal(barrier, inc=1, device_id=(g, (t + d) % times), device_id_type=MESH)
        return carry

    lax.fori_loop(1, times, greet_time, 0)

    def greet_plane(d, carry):
        pl.semaphore_signal(
            barrier, inc=1, device_id=((g + d // 2) % groups, z * 2 + d % 2), device_id_type=MESH
        )
        return carry

    lax.fori_loop(2, members, greet_plane, 0)

    for load in loads[:3]:
        load.wait()

    row = lax.broadcasted_iota(jnp.int32, (steps, steps), 0)
    col = lax.broadcasted_iota(jnp.int32, (steps, steps), 1)
    hit = col == (row % SUB) * inner + row // SUB
    back = row == (col % SUB) * inner + col // SUB
    order = jnp.where(hit, 1.0, 0.0).astype(BF16)
    restore = jnp.where(back, 1.0, 0.0).astype(BF16)
    damp = jnp.sum(jnp.where(hit, damp_ref[...], 0.0), axis=1, keepdims=True)
    dampb[:steps, :] = jnp.broadcast_to(damp, (steps, LANE))
    sig = jnp.dot(order, sig_ref[...], preferred_element_type=F32)
    cot = jnp.dot(order, cot_ref[...], preferred_element_type=F32)
    sigb[...] = sig.astype(BF16)
    cotb[...] = cot.astype(BF16)
    fsend[0] = sig.T
    fsend[1] = cot.T

    pl.semaphore_wait(barrier, (times - 1) + (members - 2))

    def place_of(kind):
        return jnp.where(kind == 0, lo, hi)

    def flipped(device, kind):
        return jnp.where(kind == 0, (device + 2) % groups, device + 1 - 2 * (device % 2))

    def pair_target(d):
        kind = c if d == 0 else 1 - c
        mine = place_of(kind)
        theirs = mine if d == 1 else 1 - mine
        device = jnp.where(kind == 0, hi * 2 + theirs, theirs * 2 + lo)
        return kind, device, mine * 2 + c

    def factor_copy(d):
        kind, device, slot = pair_target(d)
        return pltpu.make_async_remote_copy(
            src_ref=fsend.at[kind], dst_ref=fgat.at[slot],
            send_sem=fsend_sem.at[d], recv_sem=frecv_sem.at[d],
            device_id=(device, z * 2 + kind), device_id_type=MESH,
        )

    for d in (0, 2, 1):
        factor_copy(d).start()
    own_slot = place_of(c) * 2 + c
    fgat[own_slot] = fsend[c]

    for load in loads[3:]:
        load.wait()
    gamma = par_ref[2:3, :]
    x[:, :width] = gamma * jnp.dot(sigb[...], win_ref[:, :width], preferred_element_type=F32)
    x[:, width:] = gamma * jnp.dot(sigb[...], win_ref[:, width:], preferred_element_type=F32)

    lre = jnp.broadcast_to(par_ref[0:1, :], (SUB, width))
    lim = jnp.broadcast_to(par_ref[1:2, :], (SUB, width))

    def rows_of(j):
        return slice(j * SUB, (j + 1) * SUB)

    def forward_step(j, sre, sim):
        rows = rows_of(j)
        a = dampb[rows, 0:1]
        mre, mim = cmul(lre, lim, sre, sim)
        return a * mre + x[rows, :width], a * mim + x[rows, width:]

    def backward_step(j, bre, bim):
        rows = rows_of(j)
        a = dampb[rows, 0:1]
        are = y[rows, :width] + bre
        aim = y[rows, width:] + bim
        return are, aim, a * (lre * are + lim * aim), a * (lre * aim - lim * are)

    zero = jnp.zeros((SUB, width), F32)
    sre, sim = zero, zero
    for j in range(inner):
        sre, sim = forward_step(j, sre, sim)
    ends[0] = sre
    ends[1] = sim
    prod = dampb[0:SUB, :]
    for j in range(1, inner):
        prod = prod * dampb[rows_of(j), :]
    dampb[steps : steps + SUB, :] = prod

    one_re, one_im = square_times(par_ref[0:1, :], par_ref[1:2, :], inner)
    place = lax.broadcasted_iota(jnp.int32, (SUB, width), 0)

    def edge_power(index):
        pre, pim = jnp.ones((SUB, width), F32), zero
        qre, qim = one_re, one_im
        bit = 1
        while bit < SUB:
            on = (index // bit) % 2 == 1
            pre, pim = cmul(pre, pim, jnp.where(on, qre, 1.0), jnp.where(on, qim, 0.0))
            qre, qim = cmul(qre, qim, qre, qim)
            bit *= 2
        return pre, pim, qre, qim

    pre, pim, dre, dim = edge_power(place)
    tre, tim, _, _ = edge_power(SUB - 1 - place)

    ere = eim = jnp.zeros((1, width), F32)
    total = jnp.ones((1, LANE), F32)
    for o in range(SUB):
        one = slice(o, o + 1)
        enters[0, one] = ere
        enters[1, one] = eim
        dampb[steps + SUB + o : steps + SUB + o + 1, :] = total
        here = dampb[steps + o : steps + o + 1, :]
        mre, mim = cmul(one_re, one_im, ere, eim)
        ere = here[:, 0:1] * mre + ends[0, one]
        eim = here[:, 0:1] * mim + ends[1, one]
        total = total * here
    cmsg[0, 2] = jnp.broadcast_to(total, (tiles, LANE))
    cmsg[1, 2] = jnp.broadcast_to(total, (tiles, LANE))
    for i in range(tiles):
        lanes = slice(i * LANE, (i + 1) * LANE)
        one = slice(i, i + 1)
        cmsg[0, 0, one] = ere[:, lanes]
        cmsg[0, 1, one] = eim[:, lanes]

    def carry_copy(q):
        later = jnp.where(q > t, 0, 1)
        return pltpu.make_async_remote_copy(
            src_ref=cmsg.at[later], dst_ref=crecv.at[t],
            send_sem=csend_sem.at[q], recv_sem=crecv_sem.at[t],
            device_id=(g, q), device_id_type=MESH,
        )

    def carry_arrival(q):
        return pltpu.make_async_remote_copy(
            src_ref=cmsg.at[0], dst_ref=crecv.at[q],
            send_sem=csend_sem.at[q], recv_sem=crecv_sem.at[q],
            device_id=(g, q), device_id_type=MESH,
        )

    def start_carry(q, carry):
        carry_copy(q).start()
        return carry

    lax.fori_loop(t + 1, times, start_carry, 0)

    y[...] = jnp.dot(cotb[...], wout_ref[...], preferred_element_type=F32)
    bre, bim = zero, zero
    for j in reversed(range(inner)):
        _, _, bre, bim = backward_step(j, bre, bim)
    ends[2] = bre
    ends[3] = bim
    ore = oim = jnp.zeros((1, width), F32)
    tail = jnp.ones((1, LANE), F32)
    for o in reversed(range(SUB)):
        one = slice(o, o + 1)
        enters[2, one] = ore
        enters[3, one] = oim
        dampb[steps + 2 * SUB + o : steps + 2 * SUB + o + 1, :] = tail
        here = dampb[steps + o : steps + o + 1, :]
        mre = one_re * ore + one_im * oim
        mim = one_re * oim - one_im * ore
        ore = here[:, 0:1] * mre + ends[2, one]
        oim = here[:, 0:1] * mim + ends[3, one]
        tail = tail * here

    for i in range(tiles):
        lanes = slice(i * LANE, (i + 1) * LANE)
        one = slice(i, i + 1)
        cmsg[1, 0, one] = ore[:, lanes]
        cmsg[1, 1, one] = oim[:, lanes]
        ldev[0, one] = dre[:, lanes]
        ldev[1, one] = dim[:, lanes]

    lax.fori_loop(0, t, start_carry, 0)

    def ahead(q, carry):
        carry_arrival(q).wait_recv()
        mre, mim = cmul(ldev[0], ldev[1], carry[0], carry[1])
        factor_q = crecv[q, 2]
        return factor_q * mre + crecv[q, 0], factor_q * mim + crecv[q, 1]

    def behind(i, carry):
        q = times - 1 - i
        carry_arrival(q).wait_recv()
        mre = ldev[0] * carry[0] + ldev[1] * carry[1]
        mim = ldev[0] * carry[1] - ldev[1] * carry[0]
        factor_q = crecv[q, 2]
        return factor_q * mre + crecv[q, 0], factor_q * mim + crecv[q, 1]

    none = jnp.zeros((tiles, LANE), F32)
    cfull[0], cfull[1] = lax.fori_loop(0, t, ahead, (none, none))

    def wide(i):
        return jnp.concatenate([cfull[i, k : k + 1, :] for k in range(tiles)], axis=1)

    def rounded(value):
        return value.astype(BF16).astype(F32)

    mre, mim = cmul(pre, pim, wide(0), wide(1))
    reach = dampb[steps + SUB : steps + 2 * SUB, 0:1]
    sre = enters[0] + reach * mre
    sim = enters[1] + reach * mim
    for j in range(inner):
        sre, sim = forward_step(j, sre, sim)
        kre, kim = rounded(sre), rounded(sim)
        for i in range(tiles):
            lanes = slice(i * LANE, (i + 1) * LANE)
            dsend[1, i, rows_of(j)] = kre[:, lanes]
            dsend[1, tiles + i, rows_of(j)] = kim[:, lanes]

    def unit_column(u, device, kind):
        keeper = device if u % 2 else flipped(device, kind)
        return keeper * chunks + u // 2

    def drive_copy(u, d):
        kind, device, slot = pair_target(d)
        return pltpu.make_async_remote_copy(
            src_ref=dsend.at[kind, unit_column(u, device, kind)], dst_ref=dgat.at[u, slot],
            send_sem=dsend_sem.at[u, d], recv_sem=drecv_sem.at[u, d],
            device_id=(device, z * 2 + kind), device_id_type=MESH,
        )

    early = min(4, units)

    def start_drive(kind):
        @pl.when(c == kind)
        def _():
            for u in range(early):
                drive_copy(u, 0).start()

        @pl.when(c != kind)
        def _():
            for u in range(early):
                drive_copy(u, 2).start()
                drive_copy(u, 1).start()

    start_drive(1)

    cfull[2], cfull[3] = lax.fori_loop(0, times - 1 - t, behind, (none, none))
    kre, kim = wide(2), wide(3)
    mre = tre * kre + tim * kim
    mim = tre * kim - tim * kre
    reach = dampb[steps + 2 * SUB : steps + 3 * SUB, 0:1]
    bre = enters[2] + reach * mre
    bim = enters[3] + reach * mim
    for j in reversed(range(inner)):
        are, aim, bre, bim = backward_step(j, bre, bim)
        kre, kim = rounded(gamma * are), rounded(gamma * aim)
        for i in range(tiles):
            lanes = slice(i * LANE, (i + 1) * LANE)
            dsend[0, i, rows_of(j)] = kre[:, lanes]
            dsend[0, tiles + i, rows_of(j)] = kim[:, lanes]

    start_drive(0)
    for u in range(units):
        dgat[u, own_slot] = dsend[c, unit_column(u, g, c)]

    for d in range(3):
        factor_copy(d).wait_recv()
    for m in range(4):
        factor[:, m * steps : (m + 1) * steps] = fgat[m].astype(BF16)

    def partner_copy(k):
        return pltpu.make_async_remote_copy(
            src_ref=rsend.at[k], dst_ref=rgat.at[k],
            send_sem=rsend_sem.at[k], recv_sem=rrecv_sem.at[k],
            device_id=(flipped(g, c), t), device_id_type=MESH,
        )

    def plane_copy(k, d):
        other = (z + d) % planes
        return pltpu.make_async_remote_copy(
            src_ref=zsend.at[k, other], dst_ref=zgat.at[k, z],
            send_sem=zsend_sem.at[k, d], recv_sem=zrecv_sem.at[k, d],
            device_id=(g, other * 2 + c), device_id_type=MESH,
        )

    def owner_copy(k, d):
        m = (me + d) % members
        return pltpu.make_async_remote_copy(
            src_ref=osend.at[k, m], dst_ref=ogat.at[k, me],
            send_sem=osend_sem.at[k, d], recv_sem=orecv_sem.at[k, d],
            device_id=(m // 2, z * 2 + m % 2), device_id_type=MESH,
        )

    def product(u):
        for d in range(3):
            drive_copy(u, d).wait_recv()
        whole = dgat[u].reshape(4 * steps, LANE).astype(BF16)
        return jnp.dot(factor[...], whole, preferred_element_type=F32)

    def multiply(k):
        rsend[k] = product(2 * k)
        partner_copy(k).start()
        pbuf[k] = product(2 * k + 1)

    def add_partner(k):
        partner_copy(k).wait_recv()
        for gg in range(groups):
            for zz in range(planes):
                first = gg * times * own_rows + zz * pair_rows
                rows = slice(first, first + pair_rows)
                zsend[k, zz, gg * pair_rows : (gg + 1) * pair_rows] = pbuf[k, rows] + rgat[k, rows]

        def start_plane(d, carry):
            plane_copy(k, d).start()
            return carry

        lax.fori_loop(1, planes, start_plane, 0)

    def add_planes(k):
        def add_plane(d, acc):
            plane_copy(k, d).wait_recv()
            return acc + zgat[k, (z + planes - d) % planes]

        pbuf[k, : members * own_rows] = lax.fori_loop(1, planes, add_plane, zsend[k, z])
        for m in range(members):
            osend[k, m] = pbuf[k, m * own_rows : (m + 1) * own_rows]

        def start_owner(d, carry):
            owner_copy(k, d).start()
            return carry

        lax.fori_loop(1, members, start_owner, 0)
        ogat[k, me] = osend[k, me]

    def finish(k):
        def await_owner(d, carry):
            owner_copy(k, d).wait_recv()
            return carry

        lax.fori_loop(1, members, await_owner, 0)
        for gg in range(groups):
            lanes = slice((gg * chunks + k) * LANE, (gg * chunks + k + 1) * LANE)
            gin_ref[:, lanes] = ogat[k, gg * 2]
            gout_ref[:, lanes] = ogat[k, gg * 2 + 1]

    turned = (((1,), (1,)), ((), ()))

    def mix(kind, bits, weight, skipped, result):
        for i in range(2 * tiles):
            bits[:, i * LANE : (i + 1) * LANE] = dsend[kind, i].astype(BF16)
        out = lax.dot_general(bits[...], weight[...], turned, preferred_element_type=F32)
        out = (out + skip_ref[...] * skipped[...].astype(F32)).astype(BF16)
        result[...] = jnp.dot(restore, out, preferred_element_type=F32).astype(BF16)

    for s in range(chunks + 4):
        if s < chunks:
            multiply(s)
            for u in range(early + 2 * s, min(early + 2 * s + 2, units)):
                for d in (0, 2, 1):
                    drive_copy(u, d).start()
        if s == 0:
            mix(1, packed, wout_ref, sigb, mixed_ref)
        if s == min(1, chunks - 1):
            mix(0, drive, win_ref, cotb, gsig_ref)
        if 0 <= s - 1 < chunks:
            add_partner(s - 1)
        if 0 <= s - 3 < chunks:
            add_planes(s - 3)
        if 0 <= s - 4 < chunks:
            finish(s - 4)

    for d in range(3):
        factor_copy(d).wait_send()
        for u in range(units):
            drive_copy(u, d).wait_send()
    for k in range(chunks):
        partner_copy(k).wait_send()

    def drain_members(d, carry):
        for k in range(chunks):
            owner_copy(k, d).wait_send()
        return carry

    lax.fori_loop(1, members, drain_members, 0)

    def drain_planes(d, carry):
        for k in range(chunks):
            plane_copy(k, d).wait_send()
        return carry

    lax.fori_loop(1, planes, drain_planes, 0)

    def drain_times(d, carry):
        carry_copy((t + d) % times).wait_send()
        return carry

    lax.fori_loop(1, times, drain_times, 0)


def body(groups, times, signal, damping, nu_log, theta, in_weight, out_weight, skip_gain, cotangent):
    _, steps, feat = signal.shape
    width = nu_log.shape[0]
    rate = jnp.exp(nu_log)
    magnitude = jnp.exp(-rate)
    scaling = jnp.sqrt(-jnp.expm1(-2.0 * rate))
    par = jnp.stack([magnitude * jnp.cos(theta), magnitude * jnp.sin(theta), scaling], 0)
    members = groups * 2
    planes = times // 2
    block = 2 * width // groups
    chunks = block // LANE
    tiles = width // LANE
    own_rows = feat // (groups * times)
    plane_rows = feat // planes
    vmem = pl.BlockSpec(memory_space=pltpu.VMEM)
    dma = pltpu.SemaphoreType.DMA
    scratch = [
        pltpu.VMEM((steps, feat), BF16),
        pltpu.VMEM((1, steps), F32),
        pltpu.VMEM((feat, 2 * width), BF16),
        pltpu.VMEM((feat, 2 * width), BF16),
        pltpu.VMEM((1, feat), F32),
        pltpu.VMEM((steps, feat), BF16),
        dma((6,)),
        pltpu.VMEM((steps + 3 * SUB, LANE), F32),
        pltpu.VMEM((steps, feat), BF16),
        pltpu.VMEM((steps, feat), BF16),
        pltpu.VMEM((steps, 2 * width), F32),
        pltpu.VMEM((steps, 2 * width), F32),
        pltpu.VMEM((4, SUB, width), F32),
        pltpu.VMEM((4, SUB, width), F32),
        pltpu.VMEM((2, 3, tiles, LANE), F32),
        pltpu.VMEM((times, 3, tiles, LANE), F32),
        pltpu.VMEM((2, tiles, LANE), F32),
        pltpu.VMEM((4, tiles, LANE), F32),
        pltpu.VMEM((2, feat, steps), F32),
        pltpu.VMEM((4, feat, steps), F32),
        pltpu.VMEM((feat, 4 * steps), BF16),
        pltpu.VMEM((2, 2 * tiles, steps, LANE), F32),
        pltpu.VMEM((2 * chunks, 4, steps, LANE), F32),
        pltpu.VMEM((steps, 2 * width), BF16),
        pltpu.VMEM((steps, 2 * width), BF16),
        pltpu.VMEM((chunks, feat, LANE), F32),
        pltpu.VMEM((chunks, feat, LANE), F32),
        pltpu.VMEM((chunks, feat, LANE), F32),
        pltpu.VMEM((chunks, planes, plane_rows, LANE), F32),
        pltpu.VMEM((chunks, planes, plane_rows, LANE), F32),
        pltpu.VMEM((chunks, members, own_rows, LANE), F32),
        pltpu.VMEM((chunks, members, own_rows, LANE), F32),
        dma((times,)), dma((times,)),
        dma((3,)), dma((3,)),
        dma((2 * chunks, 3)), dma((2 * chunks, 3)),
        dma((chunks,)), dma((chunks,)),
        dma((chunks, planes)), dma((chunks, planes)),
        dma((chunks, members)), dma((chunks, members)),
    ]
    hbm = pl.BlockSpec(memory_space=pltpu.HBM)
    out = pl.pallas_call(
        functools.partial(kernel, groups, times),
        out_shape=(
            jax.ShapeDtypeStruct((steps, feat), BF16),
            jax.ShapeDtypeStruct((steps, feat), BF16),
            jax.ShapeDtypeStruct((own_rows, 2 * width), F32),
            jax.ShapeDtypeStruct((own_rows, 2 * width), F32),
        ),
        in_specs=[hbm, hbm, vmem, hbm, hbm, hbm, hbm],
        out_specs=(vmem,) * 4,
        scratch_shapes=scratch,
        compiler_params=pltpu.CompilerParams(
            collective_id=0, has_side_effects=True, vmem_limit_bytes=60 * 1024 * 1024
        ),
        cost_estimate=pl.CostEstimate(
            flops=14 * steps * feat * 2 * width, bytes_accessed=8 * feat * width, transcendentals=0
        ),
    )(signal[0], damping, par, in_weight, out_weight, skip_gain[None], cotangent[0])
    return (out[0][None], out[1][None], out[2], out[3])


def solution(mesh):
    placed = (P("grp", "tm", None), P("grp", "tm"), P(), P(), P(), P(), P(), P("grp", "tm", None))
    return jax.shard_map(
        functools.partial(body, mesh.shape["grp"], mesh.shape["tm"]),
        mesh=mesh,
        in_specs=placed,
        out_specs=(
            P("grp", "tm", None),
            P("grp", "tm", None),
            P(("grp", "tm"), None),
            P(("grp", "tm"), None),
        ),
        check_vma=False,
    )
```

```python
import functools

import jax
import jax.numpy as jnp
from jax import lax
from jax.experimental import pallas as pl
from jax.experimental.pallas import tpu as pltpu
from jax.sharding import PartitionSpec as P

MESH = pl.DeviceIdType.MESH
F32 = jnp.float32
BF16 = jnp.bfloat16
SUB = 8
LANE = 128


def cmul(ar, ai, br, bi):
    return ar * br - ai * bi, ar * bi + ai * br


def square_times(re, im, count):
    while count > 1:
        re, im = cmul(re, im, re, im)
        count //= 2
    return re, im


def kernel(
    groups, times,
    sig_hbm, damp_hbm, lre_ref, lim_ref, gamma_ref, win_hbm, wout_hbm, skip_hbm, cot_hbm,
    mixed_ref, gsig_ref, gin_ref, gout_ref,
    sig_ref, damp_ref, win_ref, wout_ref, skip_ref, cot_ref, load_sem,
    dampb, sigb, cotb, x, y, ends, enters, cmsg, crecv, ldev, cfull,
    fsend, fgat, factor, dsend, dgat, packed, drive, pbuf, rsend, rgat, zsend, zgat, hsend, hgat, osend, ogat,
    csend_sem, crecv_sem, fsend_sem, frecv_sem, dsend_sem, drecv_sem,
    rsend_sem, rrecv_sem, zsend_sem, zrecv_sem, osend_sem, orecv_sem,
):
    steps, feat = sig_hbm.shape
    width = lre_ref.shape[1]
    inner = steps // SUB
    planes = times // 2
    members = groups * 2
    block = 2 * width // groups
    chunks = block // LANE
    tiles = width // LANE
    own_rows = feat // (groups * times)
    pair_rows = 2 * own_rows
    units = 2 * chunks
    half = planes // 2

    g = lax.axis_index("grp")
    t = lax.axis_index("tm")
    c = t % 2
    z = t // 2
    me = g * 2 + c

    hi = g // 2
    lo = g % 2

    loads = [
        pltpu.make_async_copy(src, dst, load_sem.at[i])
        for i, (src, dst) in enumerate(
            (
                (sig_hbm, sig_ref), (cot_hbm, cot_ref), (damp_hbm, damp_ref),
                (win_hbm, win_ref), (wout_hbm, wout_ref), (skip_hbm, skip_ref),
            )
        )
    ]
    for load in loads:
        load.start()

    barrier = pltpu.get_barrier_semaphore()

    def greet_time(d, carry):
        pl.semaphore_signal(barrier, inc=1, device_id=(g, (t + d) % times), device_id_type=MESH)
        return carry

    lax.fori_loop(1, times, greet_time, 0)

    def greet_plane(d, carry):
        pl.semaphore_signal(
            barrier, inc=1, device_id=((g + d // 2) % groups, z * 2 + d % 2), device_id_type=MESH
        )
        return carry

    lax.fori_loop(2, members, greet_plane, 0)

    for load in loads[:3]:
        load.wait()

    row = lax.broadcasted_iota(jnp.int32, (steps, steps), 0)
    col = lax.broadcasted_iota(jnp.int32, (steps, steps), 1)
    hit = col == (row % SUB) * inner + row // SUB
    back = row == (col % SUB) * inner + col // SUB
    order = jnp.where(hit, 1.0, 0.0).astype(BF16)
    restore = jnp.where(back, 1.0, 0.0).astype(BF16)
    damp = jnp.sum(jnp.where(hit, damp_ref[...], 0.0), axis=1, keepdims=True)
    dampb[:steps, :] = jnp.broadcast_to(damp, (steps, LANE))
    sig = jnp.dot(order, sig_ref[...], preferred_element_type=F32)
    cot = jnp.dot(order, cot_ref[...], preferred_element_type=F32)
    sigb[...] = sig.astype(BF16)
    cotb[...] = cot.astype(BF16)
    fsend[0] = sig.T
    fsend[1] = cot.T

    pl.semaphore_wait(barrier, (times - 1) + (members - 2))

    def place_of(kind):
        return jnp.where(kind == 0, lo, hi)

    def flipped(device, kind):
        return jnp.where(kind == 0, (device + 2) % groups, device + 1 - 2 * (device % 2))

    def pair_target(d):
        kind = c if d == 0 else 1 - c
        mine = place_of(kind)
        theirs = mine if d == 1 else 1 - mine
        device = jnp.where(kind == 0, hi * 2 + theirs, theirs * 2 + lo)
        return kind, device, mine * 2 + c

    def factor_copy(d):
        kind, device, slot = pair_target(d)
        return pltpu.make_async_remote_copy(
            src_ref=fsend.at[kind], dst_ref=fgat.at[slot],
            send_sem=fsend_sem.at[d], recv_sem=frecv_sem.at[d],
            device_id=(device, z * 2 + kind), device_id_type=MESH,
        )

    for d in (0, 2, 1):
        factor_copy(d).start()
    own_slot = place_of(c) * 2 + c
    fgat[own_slot] = fsend[c]

    for load in loads[3:]:
        load.wait()
    gamma = gamma_ref[...]
    x[:, :width] = gamma * jnp.dot(sigb[...], win_ref[:, :width], preferred_element_type=F32)
    x[:, width:] = gamma * jnp.dot(sigb[...], win_ref[:, width:], preferred_element_type=F32)

    lre = jnp.broadcast_to(lre_ref[...], (SUB, width))
    lim = jnp.broadcast_to(lim_ref[...], (SUB, width))

    def rows_of(j):
        return slice(j * SUB, (j + 1) * SUB)

    def forward_step(j, sre, sim):
        rows = rows_of(j)
        a = dampb[rows, 0:1]
        mre, mim = cmul(lre, lim, sre, sim)
        return a * mre + x[rows, :width], a * mim + x[rows, width:]

    def backward_step(j, bre, bim):
        rows = rows_of(j)
        a = dampb[rows, 0:1]
        are = y[rows, :width] + bre
        aim = y[rows, width:] + bim
        return are, aim, a * (lre * are + lim * aim), a * (lre * aim - lim * are)

    zero = jnp.zeros((SUB, width), F32)
    sre, sim = zero, zero
    for j in range(inner):
        sre, sim = forward_step(j, sre, sim)
    ends[0] = sre
    ends[1] = sim
    prod = dampb[0:SUB, :]
    for j in range(1, inner):
        prod = prod * dampb[rows_of(j), :]
    dampb[steps : steps + SUB, :] = prod

    one_re, one_im = square_times(lre_ref[...], lim_ref[...], inner)
    place = lax.broadcasted_iota(jnp.int32, (SUB, width), 0)

    def edge_power(index):
        pre, pim = jnp.ones((SUB, width), F32), zero
        qre, qim = one_re, one_im
        bit = 1
        while bit < SUB:
            on = (index // bit) % 2 == 1
            pre, pim = cmul(pre, pim, jnp.where(on, qre, 1.0), jnp.where(on, qim, 0.0))
            qre, qim = cmul(qre, qim, qre, qim)
            bit *= 2
        return pre, pim, qre, qim

    pre, pim, dre, dim = edge_power(place)
    tre, tim, _, _ = edge_power(SUB - 1 - place)

    ere = eim = jnp.zeros((1, width), F32)
    total = jnp.ones((1, LANE), F32)
    for o in range(SUB):
        one = slice(o, o + 1)
        enters[0, one] = ere
        enters[1, one] = eim
        dampb[steps + SUB + o : steps + SUB + o + 1, :] = total
        here = dampb[steps + o : steps + o + 1, :]
        mre, mim = cmul(one_re, one_im, ere, eim)
        ere = here[:, 0:1] * mre + ends[0, one]
        eim = here[:, 0:1] * mim + ends[1, one]
        total = total * here
    cmsg[0, 2] = jnp.broadcast_to(total, (tiles, LANE))
    cmsg[1, 2] = jnp.broadcast_to(total, (tiles, LANE))
    for i in range(tiles):
        lanes = slice(i * LANE, (i + 1) * LANE)
        one = slice(i, i + 1)
        cmsg[0, 0, one] = ere[:, lanes]
        cmsg[0, 1, one] = eim[:, lanes]

    def carry_copy(q):
        later = jnp.where(q > t, 0, 1)
        return pltpu.make_async_remote_copy(
            src_ref=cmsg.at[later], dst_ref=crecv.at[t],
            send_sem=csend_sem.at[q], recv_sem=crecv_sem.at[t],
            device_id=(g, q), device_id_type=MESH,
        )

    def carry_arrival(q):
        return pltpu.make_async_remote_copy(
            src_ref=cmsg.at[0], dst_ref=crecv.at[q],
            send_sem=csend_sem.at[q], recv_sem=crecv_sem.at[q],
            device_id=(g, q), device_id_type=MESH,
        )

    def start_carry(q, carry):
        carry_copy(q).start()
        return carry

    lax.fori_loop(t + 1, times, start_carry, 0)

    y[...] = jnp.dot(cotb[...], wout_ref[...], preferred_element_type=F32)
    bre, bim = zero, zero
    for j in reversed(range(inner)):
        _, _, bre, bim = backward_step(j, bre, bim)
    ends[2] = bre
    ends[3] = bim
    ore = oim = jnp.zeros((1, width), F32)
    tail = jnp.ones((1, LANE), F32)
    for o in reversed(range(SUB)):
        one = slice(o, o + 1)
        enters[2, one] = ore
        enters[3, one] = oim
        dampb[steps + 2 * SUB + o : steps + 2 * SUB + o + 1, :] = tail
        here = dampb[steps + o : steps + o + 1, :]
        mre = one_re * ore + one_im * oim
        mim = one_re * oim - one_im * ore
        ore = here[:, 0:1] * mre + ends[2, one]
        oim = here[:, 0:1] * mim + ends[3, one]
        tail = tail * here

    for i in range(tiles):
        lanes = slice(i * LANE, (i + 1) * LANE)
        one = slice(i, i + 1)
        cmsg[1, 0, one] = ore[:, lanes]
        cmsg[1, 1, one] = oim[:, lanes]
        ldev[0, one] = dre[:, lanes]
        ldev[1, one] = dim[:, lanes]

    lax.fori_loop(0, t, start_carry, 0)

    def ahead(q, carry):
        carry_arrival(q).wait_recv()
        mre, mim = cmul(ldev[0], ldev[1], carry[0], carry[1])
        factor_q = crecv[q, 2]
        return factor_q * mre + crecv[q, 0], factor_q * mim + crecv[q, 1]

    def behind(i, carry):
        q = times - 1 - i
        carry_arrival(q).wait_recv()
        mre = ldev[0] * carry[0] + ldev[1] * carry[1]
        mim = ldev[0] * carry[1] - ldev[1] * carry[0]
        factor_q = crecv[q, 2]
        return factor_q * mre + crecv[q, 0], factor_q * mim + crecv[q, 1]

    none = jnp.zeros((tiles, LANE), F32)
    cfull[0], cfull[1] = lax.fori_loop(0, t, ahead, (none, none))

    def wide(i):
        return jnp.concatenate([cfull[i, k : k + 1, :] for k in range(tiles)], axis=1)

    def rounded(value):
        return value.astype(BF16).astype(F32)

    mre, mim = cmul(pre, pim, wide(0), wide(1))
    reach = dampb[steps + SUB : steps + 2 * SUB, 0:1]
    sre = enters[0] + reach * mre
    sim = enters[1] + reach * mim
    for j in range(inner):
        sre, sim = forward_step(j, sre, sim)
        kre, kim = rounded(sre), rounded(sim)
        for i in range(tiles):
            lanes = slice(i * LANE, (i + 1) * LANE)
            dsend[1, i, rows_of(j)] = kre[:, lanes]
            dsend[1, tiles + i, rows_of(j)] = kim[:, lanes]

    def unit_column(u, device, kind):
        keeper = device if u % 2 else flipped(device, kind)
        return keeper * chunks + u // 2

    def drive_copy(u, d):
        kind, device, slot = pair_target(d)
        return pltpu.make_async_remote_copy(
            src_ref=dsend.at[kind, unit_column(u, device, kind)], dst_ref=dgat.at[u, slot],
            send_sem=dsend_sem.at[u, d], recv_sem=drecv_sem.at[u, d],
            device_id=(device, z * 2 + kind), device_id_type=MESH,
        )

    early = min(4, units)

    def start_drive(kind):
        @pl.when(c == kind)
        def _():
            for u in range(early):
                drive_copy(u, 0).start()

        @pl.when(c != kind)
        def _():
            for u in range(early):
                drive_copy(u, 2).start()
                drive_copy(u, 1).start()

    start_drive(1)

    cfull[2], cfull[3] = lax.fori_loop(0, times - 1 - t, behind, (none, none))
    kre, kim = wide(2), wide(3)
    mre = tre * kre + tim * kim
    mim = tre * kim - tim * kre
    reach = dampb[steps + 2 * SUB : steps + 3 * SUB, 0:1]
    bre = enters[2] + reach * mre
    bim = enters[3] + reach * mim
    for j in reversed(range(inner)):
        are, aim, bre, bim = backward_step(j, bre, bim)
        kre, kim = rounded(gamma * are), rounded(gamma * aim)
        for i in range(tiles):
            lanes = slice(i * LANE, (i + 1) * LANE)
            dsend[0, i, rows_of(j)] = kre[:, lanes]
            dsend[0, tiles + i, rows_of(j)] = kim[:, lanes]

    start_drive(0)
    for u in range(units):
        dgat[u, own_slot] = dsend[c, unit_column(u, g, c)]

    for d in range(3):
        factor_copy(d).wait_recv()
    for m in range(4):
        factor[:, m * steps : (m + 1) * steps] = fgat[m].astype(BF16)

    def partner_copy(k):
        return pltpu.make_async_remote_copy(
            src_ref=rsend.at[k], dst_ref=rgat.at[k],
            send_sem=rsend_sem.at[k], recv_sem=rrecv_sem.at[k],
            device_id=(flipped(g, c), t), device_id_type=MESH,
        )

    parity = z % 2
    rank = z // 2

    def next_copy(k):
        return pltpu.make_async_remote_copy(
            src_ref=zsend.at[k, 1 - parity], dst_ref=zgat.at[k],
            send_sem=zsend_sem.at[k, 0], recv_sem=zrecv_sem.at[k, 0],
            device_id=(g, (rank * 2 + 1 - parity) * 2 + c), device_id_type=MESH,
        )

    def plane_copy(k, d):
        other = (rank + d) % half
        return pltpu.make_async_remote_copy(
            src_ref=hsend.at[k, other], dst_ref=hgat.at[k, rank],
            send_sem=zsend_sem.at[k, d], recv_sem=zrecv_sem.at[k, d],
            device_id=(g, (other * 2 + parity) * 2 + c), device_id_type=MESH,
        )

    def owner_copy(k, d):
        m = (me + d) % members
        return pltpu.make_async_remote_copy(
            src_ref=osend.at[k, m], dst_ref=ogat.at[k, me],
            send_sem=osend_sem.at[k, d], recv_sem=orecv_sem.at[k, d],
            device_id=(m // 2, z * 2 + m % 2), device_id_type=MESH,
        )

    def product(u):
        for d in range(3):
            drive_copy(u, d).wait_recv()
        whole = dgat[u].reshape(4 * steps, LANE).astype(BF16)
        return jnp.dot(factor[...], whole, preferred_element_type=F32)

    def multiply(k):
        rsend[k] = product(2 * k)
        partner_copy(k).start()
        pbuf[k] = product(2 * k + 1)

    def add_partner(k):
        partner_copy(k).wait_recv()
        for gg in range(groups):
            for zz in range(planes):
                first = gg * times * own_rows + zz * pair_rows
                rows = slice(first, first + pair_rows)
                place = slice(gg * pair_rows, (gg + 1) * pair_rows)
                zsend[k, zz % 2, zz // 2, place] = pbuf[k, rows] + rgat[k, rows]
        next_copy(k).start()

    def add_next(k):
        next_copy(k).wait_recv()
        hsend[k] = zsend[k, parity] + zgat[k]

        def start_plane(d, carry):
            plane_copy(k, d).start()
            return carry

        lax.fori_loop(1, half, start_plane, 0)

    def add_planes(k):
        def add_plane(d, acc):
            plane_copy(k, d).wait_recv()
            return acc + hgat[k, (rank + half - d) % half]

        pbuf[k, : members * own_rows] = lax.fori_loop(1, half, add_plane, hsend[k, rank])
        for m in range(members):
            osend[k, m] = pbuf[k, m * own_rows : (m + 1) * own_rows]

        def start_owner(d, carry):
            owner_copy(k, d).start()
            return carry

        lax.fori_loop(1, members, start_owner, 0)
        ogat[k, me] = osend[k, me]

    def finish(k):
        def await_owner(d, carry):
            owner_copy(k, d).wait_recv()
            return carry

        lax.fori_loop(1, members, await_owner, 0)
        for gg in range(groups):
            lanes = slice((gg * chunks + k) * LANE, (gg * chunks + k + 1) * LANE)
            gin_ref[:, lanes] = ogat[k, gg * 2]
            gout_ref[:, lanes] = ogat[k, gg * 2 + 1]

    turned = (((1,), (1,)), ((), ()))

    def mix(kind, bits, weight, skipped, result):
        for i in range(2 * tiles):
            bits[:, i * LANE : (i + 1) * LANE] = dsend[kind, i].astype(BF16)
        out = lax.dot_general(bits[...], weight[...], turned, preferred_element_type=F32)
        out = (out + skip_ref[...] * skipped[...].astype(F32)).astype(BF16)
        result[...] = jnp.dot(restore, out, preferred_element_type=F32).astype(BF16)

    for s in range(chunks + 4):
        if s < chunks:
            multiply(s)
            for u in range(early + 2 * s, min(early + 2 * s + 2, units)):
                for d in (0, 2, 1):
                    drive_copy(u, d).start()
        if 0 <= s - 1 < chunks:
            add_partner(s - 1)
        if 0 <= s - 2 < chunks:
            add_next(s - 2)
        if s == 0:
            mix(1, packed, wout_ref, sigb, mixed_ref)
        if s == 1:
            mix(0, drive, win_ref, cotb, gsig_ref)
        if 0 <= s - 4 < chunks:
            add_planes(s - 4)
        if 0 <= s - 5 < chunks:
            finish(s - 5)
    finish(chunks - 1)

    for d in range(3):
        factor_copy(d).wait_send()
        for u in range(units):
            drive_copy(u, d).wait_send()
    for k in range(chunks):
        partner_copy(k).wait_send()

    def drain_members(d, carry):
        for k in range(chunks):
            owner_copy(k, d).wait_send()
        return carry

    lax.fori_loop(1, members, drain_members, 0)

    def drain_planes(d, carry):
        for k in range(chunks):
            plane_copy(k, d).wait_send()
        return carry

    lax.fori_loop(1, half, drain_planes, 0)
    for k in range(chunks):
        next_copy(k).wait_send()

    def drain_times(d, carry):
        carry_copy((t + d) % times).wait_send()
        return carry

    lax.fori_loop(1, times, drain_times, 0)


def write_out(*refs):
    count = len(refs) // 2
    sources, results, sem = refs[:count], refs[count : 2 * count], refs[-1]
    copies = [
        pltpu.make_async_copy(a, b, sem.at[i]) for i, (a, b) in enumerate(zip(sources, results))
    ]
    for copy in copies:
        copy.start()
    for copy in copies:
        copy.wait()


def body(groups, times, signal, damping, nu_log, theta, in_weight, out_weight, skip_gain, cotangent):
    _, steps, feat = signal.shape
    width = nu_log.shape[0]
    rate = jnp.exp(nu_log)
    magnitude = jnp.exp(-rate)
    scaling = jnp.sqrt(-jnp.expm1(-2.0 * rate))
    lam_re = magnitude * jnp.cos(theta)
    lam_im = magnitude * jnp.sin(theta)
    members = groups * 2
    planes = times // 2
    block = 2 * width // groups
    chunks = block // LANE
    tiles = width // LANE
    own_rows = feat // (groups * times)
    plane_rows = feat // planes
    vmem = pl.BlockSpec(memory_space=pltpu.VMEM)
    dma = pltpu.SemaphoreType.DMA
    scratch = [
        pltpu.VMEM((steps, feat), BF16),
        pltpu.VMEM((1, steps), F32),
        pltpu.VMEM((feat, 2 * width), BF16),
        pltpu.VMEM((feat, 2 * width), BF16),
        pltpu.VMEM((1, feat), F32),
        pltpu.VMEM((steps, feat), BF16),
        dma((6,)),
        pltpu.VMEM((steps + 3 * SUB, LANE), F32),
        pltpu.VMEM((steps, feat), BF16),
        pltpu.VMEM((steps, feat), BF16),
        pltpu.VMEM((steps, 2 * width), F32),
        pltpu.VMEM((steps, 2 * width), F32),
        pltpu.VMEM((4, SUB, width), F32),
        pltpu.VMEM((4, SUB, width), F32),
        pltpu.VMEM((2, 3, tiles, LANE), F32),
        pltpu.VMEM((times, 3, tiles, LANE), F32),
        pltpu.VMEM((2, tiles, LANE), F32),
        pltpu.VMEM((4, tiles, LANE), F32),
        pltpu.VMEM((2, feat, steps), F32),
        pltpu.VMEM((4, feat, steps), F32),
        pltpu.VMEM((feat, 4 * steps), BF16),
        pltpu.VMEM((2, 2 * tiles, steps, LANE), F32),
        pltpu.VMEM((2 * chunks, 4, steps, LANE), F32),
        pltpu.VMEM((steps, 2 * width), BF16),
        pltpu.VMEM((steps, 2 * width), BF16),
        pltpu.VMEM((chunks, feat, LANE), F32),
        pltpu.VMEM((chunks, feat, LANE), F32),
        pltpu.VMEM((chunks, feat, LANE), F32),
        pltpu.VMEM((chunks, 2, planes // 2, plane_rows, LANE), F32),
        pltpu.VMEM((chunks, planes // 2, plane_rows, LANE), F32),
        pltpu.VMEM((chunks, planes // 2, plane_rows, LANE), F32),
        pltpu.VMEM((chunks, planes // 2, plane_rows, LANE), F32),
        pltpu.VMEM((chunks, members, own_rows, LANE), F32),
        pltpu.VMEM((chunks, members, own_rows, LANE), F32),
        dma((times,)), dma((times,)),
        dma((3,)), dma((3,)),
        dma((2 * chunks, 3)), dma((2 * chunks, 3)),
        dma((chunks,)), dma((chunks,)),
        dma((chunks, planes // 2)), dma((chunks, planes // 2)),
        dma((chunks, members)), dma((chunks, members)),
    ]
    hbm = pl.BlockSpec(memory_space=pltpu.HBM)
    out = pl.pallas_call(
        functools.partial(kernel, groups, times),
        out_shape=(
            jax.ShapeDtypeStruct((steps, feat), BF16),
            jax.ShapeDtypeStruct((steps, feat), BF16),
            jax.ShapeDtypeStruct((own_rows, 2 * width), F32),
            jax.ShapeDtypeStruct((own_rows, 2 * width), F32),
        ),
        in_specs=[hbm, hbm, vmem, vmem, vmem, hbm, hbm, hbm, hbm],
        out_specs=(vmem,) * 4,
        scratch_shapes=scratch,
        compiler_params=pltpu.CompilerParams(
            collective_id=0, has_side_effects=True, vmem_limit_bytes=60 * 1024 * 1024
        ),
        cost_estimate=pl.CostEstimate(
            flops=14 * steps * feat * 2 * width, bytes_accessed=8 * feat * width, transcendentals=0
        ),
    )(signal[0], damping, lam_re[None], lam_im[None], scaling[None], in_weight, out_weight, skip_gain[None], cotangent[0])
    anywhere = pl.BlockSpec(memory_space=pl.ANY)
    out = pl.pallas_call(
        write_out,
        out_shape=tuple(jax.ShapeDtypeStruct(a.shape, a.dtype) for a in out),
        in_specs=[anywhere] * 4,
        out_specs=(anywhere,) * 4,
        scratch_shapes=[dma((4,))],
        compiler_params=pltpu.CompilerParams(vmem_limit_bytes=60 * 1024 * 1024),
    )(*out)
    return (out[0][None], out[1][None], out[2], out[3])


def solution(mesh):
    placed = (P("grp", "tm", None), P("grp", "tm"), P(), P(), P(), P(), P(), P("grp", "tm", None))
    return jax.shard_map(
        functools.partial(body, mesh.shape["grp"], mesh.shape["tm"]),
        mesh=mesh,
        in_specs=placed,
        out_specs=(
            P("grp", "tm", None),
            P("grp", "tm", None),
            P(("grp", "tm"), None),
            P(("grp", "tm"), None),
        ),
        check_vma=False,
    )
```

```python
import functools

import jax
import jax.numpy as jnp
from jax import lax
from jax.experimental import pallas as pl
from jax.experimental.pallas import tpu as pltpu
from jax.sharding import PartitionSpec as P

MESH = pl.DeviceIdType.MESH
F32 = jnp.float32
BF16 = jnp.bfloat16
SUB = 8
LANE = 128


def cmul(ar, ai, br, bi):
    return ar * br - ai * bi, ar * bi + ai * br


def square_times(re, im, count):
    while count > 1:
        re, im = cmul(re, im, re, im)
        count //= 2
    return re, im


def kernel(
    groups, times,
    sig_hbm, damp_hbm, lre_ref, lim_ref, gamma_ref, win_hbm, wout_hbm, skip_hbm, cot_hbm,
    mixed_ref, gsig_ref, gin_ref, gout_ref,
    sig_ref, damp_ref, win_ref, wout_ref, skip_ref, cot_ref, load_sem,
    dampb, sigb, cotb, x, y, ends, enters, cmsg, crecv, ldev, cfull,
    fsend, fgat, factor, dsend, dgat, packed, drive, pbuf, rsend, rgat, zsend, zgat, hsend, hgat, osend, ogat,
    csend_sem, crecv_sem, fsend_sem, frecv_sem, dsend_sem, drecv_sem,
    rsend_sem, rrecv_sem, zsend_sem, zrecv_sem, osend_sem, orecv_sem,
):
    steps, feat = sig_hbm.shape
    width = lre_ref.shape[1]
    inner = steps // SUB
    planes = times // 2
    members = groups * 2
    block = 2 * width // groups
    chunks = block // LANE
    tiles = width // LANE
    own_rows = feat // (groups * times)
    pair_rows = 2 * own_rows
    units = 2 * chunks
    half = planes // 2

    g = lax.axis_index("grp")
    t = lax.axis_index("tm")
    c = t % 2
    z = t // 2
    me = g * 2 + c

    hi = g // 2
    lo = g % 2

    loads = [
        pltpu.make_async_copy(src, dst, load_sem.at[i])
        for i, (src, dst) in enumerate(
            (
                (sig_hbm, sig_ref), (cot_hbm, cot_ref), (damp_hbm, damp_ref),
                (win_hbm, win_ref), (wout_hbm, wout_ref), (skip_hbm, skip_ref),
            )
        )
    ]
    for load in loads:
        load.start()

    barrier = pltpu.get_barrier_semaphore()

    def greet_time(d, carry):
        pl.semaphore_signal(barrier, inc=1, device_id=(g, (t + d) % times), device_id_type=MESH)
        return carry

    lax.fori_loop(1, times, greet_time, 0)

    def greet_plane(d, carry):
        pl.semaphore_signal(
            barrier, inc=1, device_id=((g + d // 2) % groups, z * 2 + d % 2), device_id_type=MESH
        )
        return carry

    lax.fori_loop(2, members, greet_plane, 0)

    for load in loads[:3]:
        load.wait()

    row = lax.broadcasted_iota(jnp.int32, (steps, steps), 0)
    col = lax.broadcasted_iota(jnp.int32, (steps, steps), 1)
    hit = col == (row % SUB) * inner + row // SUB
    back = row == (col % SUB) * inner + col // SUB
    order = jnp.where(hit, 1.0, 0.0).astype(BF16)
    restore = jnp.where(back, 1.0, 0.0).astype(BF16)
    damp = jnp.sum(jnp.where(hit, damp_ref[...], 0.0), axis=1, keepdims=True)
    dampb[:steps, :] = jnp.broadcast_to(damp, (steps, LANE))
    sig = jnp.dot(order, sig_ref[...], preferred_element_type=F32)
    cot = jnp.dot(order, cot_ref[...], preferred_element_type=F32)
    sigb[...] = sig.astype(BF16)
    cotb[...] = cot.astype(BF16)
    fsend[0] = sig.T
    fsend[1] = cot.T

    pl.semaphore_wait(barrier, (times - 1) + (members - 2))

    def place_of(kind):
        return jnp.where(kind == 0, lo, hi)

    def flipped(device, kind):
        return jnp.where(kind == 0, (device + 2) % groups, device + 1 - 2 * (device % 2))

    def pair_target(d):
        kind = c if d == 0 else 1 - c
        mine = place_of(kind)
        theirs = mine if d == 1 else 1 - mine
        device = jnp.where(kind == 0, hi * 2 + theirs, theirs * 2 + lo)
        return kind, device, mine * 2 + c

    def factor_copy(d):
        kind, device, slot = pair_target(d)
        return pltpu.make_async_remote_copy(
            src_ref=fsend.at[kind], dst_ref=fgat.at[slot],
            send_sem=fsend_sem.at[d], recv_sem=frecv_sem.at[d],
            device_id=(device, z * 2 + kind), device_id_type=MESH,
        )

    for d in (0, 2, 1):
        factor_copy(d).start()
    own_slot = place_of(c) * 2 + c
    fgat[own_slot] = fsend[c]

    for load in loads[3:]:
        load.wait()
    gamma = gamma_ref[...]
    x[:, :width] = gamma * jnp.dot(sigb[...], win_ref[:, :width], preferred_element_type=F32)
    x[:, width:] = gamma * jnp.dot(sigb[...], win_ref[:, width:], preferred_element_type=F32)

    lre = jnp.broadcast_to(lre_ref[...], (SUB, width))
    lim = jnp.broadcast_to(lim_ref[...], (SUB, width))

    def rows_of(j):
        return slice(j * SUB, (j + 1) * SUB)

    def forward_step(j, sre, sim):
        rows = rows_of(j)
        a = dampb[rows, 0:1]
        mre, mim = cmul(lre, lim, sre, sim)
        return a * mre + x[rows, :width], a * mim + x[rows, width:]

    def backward_step(j, bre, bim):
        rows = rows_of(j)
        a = dampb[rows, 0:1]
        are = y[rows, :width] + bre
        aim = y[rows, width:] + bim
        return are, aim, a * (lre * are + lim * aim), a * (lre * aim - lim * are)

    zero = jnp.zeros((SUB, width), F32)
    sre, sim = zero, zero
    for j in range(inner):
        sre, sim = forward_step(j, sre, sim)
    ends[0] = sre
    ends[1] = sim
    prod = dampb[0:SUB, :]
    for j in range(1, inner):
        prod = prod * dampb[rows_of(j), :]
    dampb[steps : steps + SUB, :] = prod

    one_re, one_im = square_times(lre_ref[...], lim_ref[...], inner)
    place = lax.broadcasted_iota(jnp.int32, (SUB, width), 0)

    def edge_power(index):
        pre, pim = jnp.ones((SUB, width), F32), zero
        qre, qim = one_re, one_im
        bit = 1
        while bit < SUB:
            on = (index // bit) % 2 == 1
            pre, pim = cmul(pre, pim, jnp.where(on, qre, 1.0), jnp.where(on, qim, 0.0))
            qre, qim = cmul(qre, qim, qre, qim)
            bit *= 2
        return pre, pim, qre, qim

    pre, pim, dre, dim = edge_power(place)
    tre, tim, _, _ = edge_power(SUB - 1 - place)

    ere = eim = jnp.zeros((1, width), F32)
    total = jnp.ones((1, LANE), F32)
    for o in range(SUB):
        one = slice(o, o + 1)
        enters[0, one] = ere
        enters[1, one] = eim
        dampb[steps + SUB + o : steps + SUB + o + 1, :] = total
        here = dampb[steps + o : steps + o + 1, :]
        mre, mim = cmul(one_re, one_im, ere, eim)
        ere = here[:, 0:1] * mre + ends[0, one]
        eim = here[:, 0:1] * mim + ends[1, one]
        total = total * here
    cmsg[0, 2] = jnp.broadcast_to(total, (tiles, LANE))
    cmsg[1, 2] = jnp.broadcast_to(total, (tiles, LANE))
    for i in range(tiles):
        lanes = slice(i * LANE, (i + 1) * LANE)
        one = slice(i, i + 1)
        cmsg[0, 0, one] = ere[:, lanes]
        cmsg[0, 1, one] = eim[:, lanes]

    def carry_copy(q):
        later = jnp.where(q > t, 0, 1)
        return pltpu.make_async_remote_copy(
            src_ref=cmsg.at[later], dst_ref=crecv.at[t],
            send_sem=csend_sem.at[q], recv_sem=crecv_sem.at[t],
            device_id=(g, q), device_id_type=MESH,
        )

    def carry_arrival(q):
        return pltpu.make_async_remote_copy(
            src_ref=cmsg.at[0], dst_ref=crecv.at[q],
            send_sem=csend_sem.at[q], recv_sem=crecv_sem.at[q],
            device_id=(g, q), device_id_type=MESH,
        )

    def start_carry(q, carry):
        carry_copy(q).start()
        return carry

    lax.fori_loop(t + 1, times, start_carry, 0)

    y[...] = jnp.dot(cotb[...], wout_ref[...], preferred_element_type=F32)
    bre, bim = zero, zero
    for j in reversed(range(inner)):
        _, _, bre, bim = backward_step(j, bre, bim)
    ends[2] = bre
    ends[3] = bim
    ore = oim = jnp.zeros((1, width), F32)
    tail = jnp.ones((1, LANE), F32)
    for o in reversed(range(SUB)):
        one = slice(o, o + 1)
        enters[2, one] = ore
        enters[3, one] = oim
        dampb[steps + 2 * SUB + o : steps + 2 * SUB + o + 1, :] = tail
        here = dampb[steps + o : steps + o + 1, :]
        mre = one_re * ore + one_im * oim
        mim = one_re * oim - one_im * ore
        ore = here[:, 0:1] * mre + ends[2, one]
        oim = here[:, 0:1] * mim + ends[3, one]
        tail = tail * here

    for i in range(tiles):
        lanes = slice(i * LANE, (i + 1) * LANE)
        one = slice(i, i + 1)
        cmsg[1, 0, one] = ore[:, lanes]
        cmsg[1, 1, one] = oim[:, lanes]
        ldev[0, one] = dre[:, lanes]
        ldev[1, one] = dim[:, lanes]

    lax.fori_loop(0, t, start_carry, 0)

    def ahead(q, carry):
        carry_arrival(q).wait_recv()
        mre, mim = cmul(ldev[0], ldev[1], carry[0], carry[1])
        factor_q = crecv[q, 2]
        return factor_q * mre + crecv[q, 0], factor_q * mim + crecv[q, 1]

    def behind(i, carry):
        q = times - 1 - i
        carry_arrival(q).wait_recv()
        mre = ldev[0] * carry[0] + ldev[1] * carry[1]
        mim = ldev[0] * carry[1] - ldev[1] * carry[0]
        factor_q = crecv[q, 2]
        return factor_q * mre + crecv[q, 0], factor_q * mim + crecv[q, 1]

    none = jnp.zeros((tiles, LANE), F32)
    cfull[0], cfull[1] = lax.fori_loop(0, t, ahead, (none, none))

    def wide(i):
        return jnp.concatenate([cfull[i, k : k + 1, :] for k in range(tiles)], axis=1)

    def rounded(value):
        return value.astype(BF16).astype(F32)

    mre, mim = cmul(pre, pim, wide(0), wide(1))
    reach = dampb[steps + SUB : steps + 2 * SUB, 0:1]
    sre = enters[0] + reach * mre
    sim = enters[1] + reach * mim
    for j in range(inner):
        sre, sim = forward_step(j, sre, sim)
        kre, kim = rounded(sre), rounded(sim)
        for i in range(tiles):
            lanes = slice(i * LANE, (i + 1) * LANE)
            dsend[1, i, rows_of(j)] = kre[:, lanes]
            dsend[1, tiles + i, rows_of(j)] = kim[:, lanes]

    def unit_column(u, device, kind):
        keeper = device if u % 2 else flipped(device, kind)
        return keeper * chunks + u // 2

    def drive_copy(u, d):
        kind, device, slot = pair_target(d)
        return pltpu.make_async_remote_copy(
            src_ref=dsend.at[kind, unit_column(u, device, kind)], dst_ref=dgat.at[u, slot],
            send_sem=dsend_sem.at[u, d], recv_sem=drecv_sem.at[u, d],
            device_id=(device, z * 2 + kind), device_id_type=MESH,
        )

    early = min(4, units)

    def start_drive(kind):
        @pl.when(c == kind)
        def _():
            for u in range(early):
                drive_copy(u, 0).start()

        @pl.when(c != kind)
        def _():
            for u in range(early):
                drive_copy(u, 2).start()
                drive_copy(u, 1).start()

    start_drive(1)

    cfull[2], cfull[3] = lax.fori_loop(0, times - 1 - t, behind, (none, none))
    kre, kim = wide(2), wide(3)
    mre = tre * kre + tim * kim
    mim = tre * kim - tim * kre
    reach = dampb[steps + 2 * SUB : steps + 3 * SUB, 0:1]
    bre = enters[2] + reach * mre
    bim = enters[3] + reach * mim
    for j in reversed(range(inner)):
        are, aim, bre, bim = backward_step(j, bre, bim)
        kre, kim = rounded(gamma * are), rounded(gamma * aim)
        for i in range(tiles):
            lanes = slice(i * LANE, (i + 1) * LANE)
            dsend[0, i, rows_of(j)] = kre[:, lanes]
            dsend[0, tiles + i, rows_of(j)] = kim[:, lanes]

    start_drive(0)
    for u in range(units):
        dgat[u, own_slot] = dsend[c, unit_column(u, g, c)]

    for d in range(3):
        factor_copy(d).wait_recv()
    for m in range(4):
        factor[:, m * steps : (m + 1) * steps] = fgat[m].astype(BF16)

    def partner_copy(k):
        return pltpu.make_async_remote_copy(
            src_ref=rsend.at[k], dst_ref=rgat.at[k],
            send_sem=rsend_sem.at[k], recv_sem=rrecv_sem.at[k],
            device_id=(flipped(g, c), t), device_id_type=MESH,
        )

    parity = z % 2
    rank = z // 2

    def next_copy(k):
        return pltpu.make_async_remote_copy(
            src_ref=zsend.at[k, 1 - parity], dst_ref=zgat.at[k],
            send_sem=zsend_sem.at[k, 0], recv_sem=zrecv_sem.at[k, 0],
            device_id=(g, (rank * 2 + 1 - parity) * 2 + c), device_id_type=MESH,
        )

    def plane_copy(k, d):
        other = (rank + d) % half
        return pltpu.make_async_remote_copy(
            src_ref=hsend.at[k, other], dst_ref=hgat.at[k, rank],
            send_sem=zsend_sem.at[k, d], recv_sem=zrecv_sem.at[k, d],
            device_id=(g, (other * 2 + parity) * 2 + c), device_id_type=MESH,
        )

    def owner_copy(k, d):
        m = (me + d) % members
        return pltpu.make_async_remote_copy(
            src_ref=osend.at[k, m], dst_ref=ogat.at[k, me],
            send_sem=osend_sem.at[k, d], recv_sem=orecv_sem.at[k, d],
            device_id=(m // 2, z * 2 + m % 2), device_id_type=MESH,
        )

    def product(u):
        for d in range(3):
            drive_copy(u, d).wait_recv()
        whole = dgat[u].reshape(4 * steps, LANE).astype(BF16)
        return jnp.dot(factor[...], whole, preferred_element_type=F32)

    def multiply(k):
        rsend[k] = product(2 * k)
        partner_copy(k).start()
        pbuf[k] = product(2 * k + 1)

    def add_partner(k):
        partner_copy(k).wait_recv()
        for gg in range(groups):
            for zz in range(planes):
                first = gg * times * own_rows + zz * pair_rows
                rows = slice(first, first + pair_rows)
                place = slice(gg * pair_rows, (gg + 1) * pair_rows)
                zsend[k, zz % 2, zz // 2, place] = pbuf[k, rows] + rgat[k, rows]
        next_copy(k).start()

    def add_next(k):
        next_copy(k).wait_recv()
        hsend[k] = zsend[k, parity] + zgat[k]

        def start_plane(d, carry):
            plane_copy(k, d).start()
            return carry

        lax.fori_loop(1, half, start_plane, 0)

    def add_planes(k):
        def add_plane(d, acc):
            plane_copy(k, d).wait_recv()
            return acc + hgat[k, (rank + half - d) % half]

        pbuf[k, : members * own_rows] = lax.fori_loop(1, half, add_plane, hsend[k, rank])
        for m in range(members):
            osend[k, m] = pbuf[k, m * own_rows : (m + 1) * own_rows]

        def start_owner(d, carry):
            owner_copy(k, d).start()
            return carry

        lax.fori_loop(1, members, start_owner, 0)
        ogat[k, me] = osend[k, me]

    def finish(k):
        def await_owner(d, carry):
            owner_copy(k, d).wait_recv()
            return carry

        lax.fori_loop(1, members, await_owner, 0)
        for gg in range(groups):
            lanes = slice((gg * chunks + k) * LANE, (gg * chunks + k + 1) * LANE)
            gin_ref[:, lanes] = ogat[k, gg * 2]
            gout_ref[:, lanes] = ogat[k, gg * 2 + 1]

    turned = (((1,), (1,)), ((), ()))

    def mix(kind, bits, weight, skipped, result):
        for i in range(2 * tiles):
            bits[:, i * LANE : (i + 1) * LANE] = dsend[kind, i].astype(BF16)
        out = lax.dot_general(bits[...], weight[...], turned, preferred_element_type=F32)
        out = (out + skip_ref[...] * skipped[...].astype(F32)).astype(BF16)
        result[...] = jnp.dot(restore, out, preferred_element_type=F32).astype(BF16)

    for s in range(chunks + 4):
        if s < chunks:
            multiply(s)
            for u in range(early + 2 * s, min(early + 2 * s + 2, units)):
                for d in (0, 2, 1):
                    drive_copy(u, d).start()
        if 0 <= s - 1 < chunks:
            add_partner(s - 1)
        if 0 <= s - 2 < chunks:
            add_next(s - 2)
        if s == 0:
            mix(1, packed, wout_ref, sigb, mixed_ref)
        if s == 1:
            mix(0, drive, win_ref, cotb, gsig_ref)
        if 0 <= s - 4 < chunks:
            add_planes(s - 4)
        if 0 <= s - 5 < chunks:
            finish(s - 5)
    finish(chunks - 1)

    for d in range(3):
        factor_copy(d).wait_send()
        for u in range(units):
            drive_copy(u, d).wait_send()
    for k in range(chunks):
        partner_copy(k).wait_send()

    def drain_members(d, carry):
        for k in range(chunks):
            owner_copy(k, d).wait_send()
        return carry

    lax.fori_loop(1, members, drain_members, 0)

    def drain_planes(d, carry):
        for k in range(chunks):
            plane_copy(k, d).wait_send()
        return carry

    lax.fori_loop(1, half, drain_planes, 0)
    for k in range(chunks):
        next_copy(k).wait_send()

    def drain_times(d, carry):
        carry_copy((t + d) % times).wait_send()
        return carry

    lax.fori_loop(1, times, drain_times, 0)


def write_out(*refs):
    count = len(refs) // 2
    for source, result in zip(refs[:count], refs[count:]):
        result[...] = source[...]


def body(groups, times, signal, damping, nu_log, theta, in_weight, out_weight, skip_gain, cotangent):
    _, steps, feat = signal.shape
    width = nu_log.shape[0]
    rate = jnp.exp(nu_log)
    magnitude = jnp.exp(-rate)
    scaling = jnp.sqrt(-jnp.expm1(-2.0 * rate))
    lam_re = magnitude * jnp.cos(theta)
    lam_im = magnitude * jnp.sin(theta)
    members = groups * 2
    planes = times // 2
    block = 2 * width // groups
    chunks = block // LANE
    tiles = width // LANE
    own_rows = feat // (groups * times)
    plane_rows = feat // planes
    vmem = pl.BlockSpec(memory_space=pltpu.VMEM)
    dma = pltpu.SemaphoreType.DMA
    scratch = [
        pltpu.VMEM((steps, feat), BF16),
        pltpu.VMEM((1, steps), F32),
        pltpu.VMEM((feat, 2 * width), BF16),
        pltpu.VMEM((feat, 2 * width), BF16),
        pltpu.VMEM((1, feat), F32),
        pltpu.VMEM((steps, feat), BF16),
        dma((6,)),
        pltpu.VMEM((steps + 3 * SUB, LANE), F32),
        pltpu.VMEM((steps, feat), BF16),
        pltpu.VMEM((steps, feat), BF16),
        pltpu.VMEM((steps, 2 * width), F32),
        pltpu.VMEM((steps, 2 * width), F32),
        pltpu.VMEM((4, SUB, width), F32),
        pltpu.VMEM((4, SUB, width), F32),
        pltpu.VMEM((2, 3, tiles, LANE), F32),
        pltpu.VMEM((times, 3, tiles, LANE), F32),
        pltpu.VMEM((2, tiles, LANE), F32),
        pltpu.VMEM((4, tiles, LANE), F32),
        pltpu.VMEM((2, feat, steps), F32),
        pltpu.VMEM((4, feat, steps), F32),
        pltpu.VMEM((feat, 4 * steps), BF16),
        pltpu.VMEM((2, 2 * tiles, steps, LANE), F32),
        pltpu.VMEM((2 * chunks, 4, steps, LANE), F32),
        pltpu.VMEM((steps, 2 * width), BF16),
        pltpu.VMEM((steps, 2 * width), BF16),
        pltpu.VMEM((chunks, feat, LANE), F32),
        pltpu.VMEM((chunks, feat, LANE), F32),
        pltpu.VMEM((chunks, feat, LANE), F32),
        pltpu.VMEM((chunks, 2, planes // 2, plane_rows, LANE), F32),
        pltpu.VMEM((chunks, planes // 2, plane_rows, LANE), F32),
        pltpu.VMEM((chunks, planes // 2, plane_rows, LANE), F32),
        pltpu.VMEM((chunks, planes // 2, plane_rows, LANE), F32),
        pltpu.VMEM((chunks, members, own_rows, LANE), F32),
        pltpu.VMEM((chunks, members, own_rows, LANE), F32),
        dma((times,)), dma((times,)),
        dma((3,)), dma((3,)),
        dma((2 * chunks, 3)), dma((2 * chunks, 3)),
        dma((chunks,)), dma((chunks,)),
        dma((chunks, planes // 2)), dma((chunks, planes // 2)),
        dma((chunks, members)), dma((chunks, members)),
    ]
    hbm = pl.BlockSpec(memory_space=pltpu.HBM)
    out = pl.pallas_call(
        functools.partial(kernel, groups, times),
        out_shape=(
            jax.ShapeDtypeStruct((steps, feat), BF16),
            jax.ShapeDtypeStruct((steps, feat), BF16),
            jax.ShapeDtypeStruct((own_rows, 2 * width), F32),
            jax.ShapeDtypeStruct((own_rows, 2 * width), F32),
        ),
        in_specs=[hbm, hbm, vmem, vmem, vmem, hbm, hbm, hbm, hbm],
        out_specs=(vmem,) * 4,
        scratch_shapes=scratch,
        compiler_params=pltpu.CompilerParams(
            collective_id=0, has_side_effects=True, vmem_limit_bytes=60 * 1024 * 1024
        ),
        cost_estimate=pl.CostEstimate(
            flops=14 * steps * feat * 2 * width, bytes_accessed=8 * feat * width, transcendentals=0
        ),
    )(signal[0], damping, lam_re[None], lam_im[None], scaling[None], in_weight, out_weight, skip_gain[None], cotangent[0])
    out = pl.pallas_call(
        write_out,
        out_shape=tuple(jax.ShapeDtypeStruct(a.shape, a.dtype) for a in out),
        in_specs=[vmem] * 4,
        out_specs=(vmem,) * 4,
        compiler_params=pltpu.CompilerParams(vmem_limit_bytes=60 * 1024 * 1024),
    )(*out)
    return (out[0][None], out[1][None], out[2], out[3])


def solution(mesh):
    placed = (P("grp", "tm", None), P("grp", "tm"), P(), P(), P(), P(), P(), P("grp", "tm", None))
    return jax.shard_map(
        functools.partial(body, mesh.shape["grp"], mesh.shape["tm"]),
        mesh=mesh,
        in_specs=placed,
        out_specs=(
            P("grp", "tm", None),
            P("grp", "tm", None),
            P(("grp", "tm"), None),
            P(("grp", "tm"), None),
        ),
        check_vma=False,
    )
```
